128 devices in a mesh: seq: 32 (over z, y_lo, x), chan: 4 (over y_hi, core).
Axes of the slice: x: 4, y: 4 (y_hi: 2, y_lo: 2; y = y_hi * 2 + y_lo), z: 4, core: 2. Of those that a mesh axis runs over, the one named last changes fastest.
Arguments:
- layer_in: bfloat16 [16384, 2048], P('seq', 'chan')
- factor_one: bfloat16 [64, 256, 256], P('seq'), may hold values from -0.375 to 0.375
- factor_two: bfloat16 [256, 64, 64], P('seq'), may hold values from -0.75 to 0.75
- gate_scale: float32 [2048], P('chan'), may hold values from 0.5 to 2
- gate_shift: float32 [2048], P('chan'), may hold values from -3 to 3
- norm_gain: float32 [2048], replicated, may hold values from 0.1 to 1.9
- w_gate: bfloat16 [2048, 4096], P(None, 'chan'), may hold values from -0.125 to 0.125
- w_up: bfloat16 [2048, 4096], P(None, 'chan'), may hold values from -0.125 to 0.125
- w_down: bfloat16 [4096, 2048], P('chan'), may hold values from -0.09375 to 0.09375
- out_grad: bfloat16 [16384, 2048], P('seq', 'chan'), may hold values from -6 to 6
Outputs:
- layer_out: bfloat16 [16384, 2048], P('seq', 'chan')
- input_grad: bfloat16 [16384, 2048], P('seq', 'chan')
- one_grad: float32 [64, 256, 256], P('seq')
- two_grad: float32 [256, 64, 64], P('seq')
- scale_grad: float32 [2048], P('chan')
- shift_grad: float32 [2048], P('chan')
- gain_grad: float32 [2048], P('chan')
- gate_grad: float32 [2048, 4096], P('seq', 'chan')
- up_grad: float32 [2048, 4096], P('seq', 'chan')
- down_grad: float32 [4096, 2048], P('chan', 'seq')
The draws below stay inside these ranges and needn't reach their ends.
All inputs are finite; a program needn't handle non-finite values.
Results may differ from the reference program's by a relative error of at most 0.015.
Values may be sent and summed in bfloat16 or wider, within the bound.
A program may use at most 192 MiB of HBM per device.

```python
import jax
import jax.numpy as jnp
from jax import lax

D = 2048
FF = 4096
Q = 256
LENGTH = 16384
BLOCKS = 64


def draw_layer_in(key, part):
    key = jax.random.fold_in(key, 11)
    key_rows, key_cols, key_base = jax.random.split(key, 3)
    row_scale = jnp.exp(jax.random.uniform(key_rows, (LENGTH, 1), jnp.float32, -1.2, 1.2))
    col_scale = jnp.exp(jax.random.uniform(key_cols, (1, D), jnp.float32, -1.2, 1.2))
    base = jnp.clip(jax.random.normal(key_base, (LENGTH, D), jnp.float32), -5.0, 5.0)
    values = base * row_scale * col_scale
    return values.astype(jnp.bfloat16)


def strengthened(array, rng, source, target, parts, factor):
    owner, partner = [(jnp.arange(array.shape[position]) // (array.shape[position] // parts)).reshape([-1 if axis == position else 1 for axis in range(array.ndim)]) for position in (source, target)]
    chosen = jax.random.permutation(rng, parts)[partner]
    strong = (owner == chosen) | (owner == (partner + parts // 2) % parts)
    return jnp.where(strong, factor * array, array)


def steps_of(key, extent, shards, least, top_value):
    loudness, own = 1.0, jax.random.fold_in(key, 6)
    for dim, blocks in shards:
        heights = jnp.exp(jax.random.uniform(jax.random.fold_in(own, dim), (blocks,), jnp.float32, least / len(shards), top_value / len(shards)))
        loudness = loudness * jnp.repeat(heights, extent[dim] // blocks).reshape([-1 if axis == dim else 1 for axis in range(len(extent))])
    return loudness


def gaussian(own_key, extent, width, most, pieces=(), dtype=jnp.bfloat16):
    gain = steps_of(own_key, extent, pieces, -0.22, 0.18) if pieces else 1.0
    values = jax.random.normal(own_key, extent, jnp.float32) * width * gain
    return jnp.minimum(jnp.maximum(values, -most), most).astype(dtype)


def noise_with(key, extent, scale, most, cuts, heavy, dtype=jnp.bfloat16):
    drawn = scale * jax.random.normal(key, extent, jnp.float32)
    if cuts:
        drawn = drawn * steps_of(key, extent, cuts, -0.22, 0.18)
    return jnp.clip(strengthened(drawn, jax.random.fold_in(key, 3), *heavy), -most, most).astype(dtype)


def setup_inputs(seed: int = 0) -> dict:
    keys = jax.random.split(jax.random.key(seed), 11)
    return {
        "layer_in": draw_layer_in(jax.random.fold_in(keys[10], 71), 0),
        "factor_one": gaussian(keys[1], (BLOCKS, Q, Q), Q ** -0.5, 0.375, ((0, 32),)),
        "factor_two": gaussian(keys[2], (Q, BLOCKS, BLOCKS), BLOCKS ** -0.5, 0.75, ((0, 32),)),
        "gate_scale": jnp.clip(0.5 + 1.5 * jax.random.uniform(keys[3], (D,), jnp.float32) ** steps_of(keys[3], (D,), ((0, 4),), -0.2, 0.2), 0.5, 2.0),
        "gate_shift": gaussian(keys[4], (D,), 1.0, 3.0, ((0, 4),), jnp.float32),
        "norm_gain": jnp.clip(1.0 + 0.18 * jax.random.normal(keys[5], (D,), jnp.float32), 0.1, 1.9),
        "w_gate": gaussian(keys[6], (D, FF), D ** -0.5, 0.125, ((1, 4),)),
        "w_up": gaussian(keys[7], (D, FF), D ** -0.5, 0.125, ((1, 4),)),
        "w_down": gaussian(keys[8], (FF, D), FF ** -0.5, 0.09375, ((0, 4),)),
        "out_grad": noise_with(keys[9], (LENGTH, D), 1.0, 6.0, ((0, 32), (1, 4)), (0, 1, 32, 2.75)),
    }


def reference(layer_in, factor_one, factor_two, gate_scale, gate_shift, norm_gain, w_gate, w_up, w_down, out_grad):
    in_float = layer_in.astype(jnp.float32)
    in_blocks = in_float.reshape(BLOCKS, Q, D)
    one_float = factor_one.astype(jnp.float32)
    two_float = factor_two.astype(jnp.float32)
    first = jnp.einsum('pkq,pqc->pkc', one_float, in_blocks).astype(jnp.bfloat16)
    first_float = first.astype(jnp.float32)
    second = jnp.einsum('qjp,pqc->jqc', two_float, first_float).astype(jnp.bfloat16)
    seqmix = second.astype(jnp.float32).reshape(LENGTH, D)
    opening = jax.nn.sigmoid(in_float * gate_scale + gate_shift)
    mixed = (in_float + opening * seqmix).astype(jnp.bfloat16)
    mixed_float = mixed.astype(jnp.float32)
    inv_rms = lax.rsqrt(lax.optimization_barrier(jnp.mean(mixed_float * mixed_float, axis=1, keepdims=True)) + 1e-05)
    normed = (mixed_float * inv_rms * norm_gain).astype(jnp.bfloat16)
    gate_pre = jnp.dot(normed, w_gate, preferred_element_type=jnp.float32)
    up_pre = jnp.dot(normed, w_up, preferred_element_type=jnp.float32)
    gate_sigmoid = jax.nn.sigmoid(gate_pre)
    hidden = (gate_pre * gate_sigmoid * up_pre).astype(jnp.bfloat16)
    mlp_out = jnp.dot(hidden, w_down, preferred_element_type=jnp.float32)
    layer_out = (mixed_float + mlp_out).astype(jnp.bfloat16)
    hidden_grad = jnp.dot(out_grad, w_down.T, preferred_element_type=jnp.float32)
    gate_back = (hidden_grad * up_pre * gate_sigmoid * (1.0 + gate_pre * (1.0 - gate_sigmoid))).astype(jnp.bfloat16)
    up_back = (hidden_grad * gate_pre * gate_sigmoid).astype(jnp.bfloat16)
    normed_grad = jnp.dot(gate_back, w_gate.T, preferred_element_type=jnp.float32)
    normed_grad = normed_grad + jnp.dot(up_back, w_up.T, preferred_element_type=jnp.float32)
    row_dots = lax.optimization_barrier(jnp.sum(normed_grad * norm_gain * mixed_float, axis=1, keepdims=True))
    mixed_grad = out_grad.astype(jnp.float32) + inv_rms * norm_gain * normed_grad
    mixed_grad = mixed_grad - mixed_float * inv_rms * inv_rms * inv_rms * row_dots / D
    gain_grad = lax.optimization_barrier(jnp.sum(normed_grad * mixed_float * inv_rms, axis=0))
    seqmix_grad = (mixed_grad * opening).astype(jnp.bfloat16)
    pre_grad = mixed_grad * seqmix * opening * (1.0 - opening)
    scale_grad = lax.optimization_barrier(jnp.sum(pre_grad * in_float, axis=0))
    shift_grad = lax.optimization_barrier(jnp.sum(pre_grad, axis=0))
    back_blocks = seqmix_grad.astype(jnp.float32).reshape(BLOCKS, Q, D)
    first_grad = jnp.einsum('qjp,jqc->pqc', two_float, back_blocks).astype(jnp.bfloat16)
    two_grad = jnp.einsum('jqc,pqc->qjp', back_blocks, first_float)
    first_grad_float = first_grad.astype(jnp.float32)
    input_part = jnp.einsum('pkq,pkc->pqc', one_float, first_grad_float).reshape(LENGTH, D)
    one_grad = jnp.einsum('pkc,pqc->pkq', first_grad_float, in_blocks)
    input_grad = (mixed_grad + pre_grad * gate_scale + input_part).astype(jnp.bfloat16)
    gate_grad = jnp.dot(normed.T, gate_back, preferred_element_type=jnp.float32)
    up_grad = jnp.dot(normed.T, up_back, preferred_element_type=jnp.float32)
    down_grad = jnp.dot(hidden.T, out_grad, preferred_element_type=jnp.float32)
    return (layer_out, input_grad, one_grad, two_grad, scale_grad, shift_grad, gain_grad, gate_grad, up_grad, down_grad)
```

```python
import functools

import jax
import jax.numpy as jnp
from jax import lax
from jax.experimental import pallas as pl
from jax.experimental.pallas import tpu as pltpu
from jax.sharding import PartitionSpec as P

MESH = pl.DeviceIdType.MESH
PARTS = 32
SLAB = 16
ROWS = 512
PIECES = 4
PIECE = ROWS // PIECES


def interleaved(low, high):
    pair = [part.reshape(PARTS, 8, part.shape[1]) for part in (low, high)]
    return jnp.stack(pair, axis=1).reshape(ROWS, low.shape[1])


def dot(a, b):
    return jnp.dot(a, b, preferred_element_type=jnp.float32)


def place():
    return lax.axis_index("seq"), lax.axis_index("chan")


def greet():
    s, c = place()
    barrier = pltpu.get_barrier_semaphore()

    def greet_seq(step, carry):
        target = (lax.rem(s + step, PARTS), c)
        pl.semaphore_signal(barrier, inc=1, device_id=target, device_id_type=MESH)
        return carry

    lax.fori_loop(1, PARTS, greet_seq, 0)
    for step in range(1, 4):
        target = (s, lax.rem(c + step, 4))
        pl.semaphore_signal(barrier, inc=1, device_id=target, device_id_type=MESH)
    pl.semaphore_wait(barrier, PARTS - 1 + 3)


def slab(index):
    return pl.ds(pl.multiple_of(index * SLAB, SLAB), SLAB)


def swap_start(src, dst, send, recv):
    s, c = place()

    def one(step, carry):
        target = lax.rem(s + step, PARTS)
        pltpu.make_async_remote_copy(
            src_ref=src.at[slab(target)],
            dst_ref=dst.at[slab(s)],
            send_sem=send,
            recv_sem=recv,
            device_id=(target, c),
            device_id_type=MESH,
        ).start()
        return carry

    lax.fori_loop(1, PARTS, one, 0)
    dst[slab(s), :] = src[slab(s), :]


def swap_wait(src, dst, send, recv):
    s, c = place()
    most = pl.ds(0, ROWS - SLAB)
    pltpu.make_async_remote_copy(
        src_ref=src.at[most],
        dst_ref=dst.at[most],
        send_sem=send,
        recv_sem=recv,
        device_id=(lax.rem(s + 1, PARTS), c),
        device_id_type=MESH,
    ).wait()


def chan_copy(buf, owner, piece, lane, send, recv, target):
    part = buf.at[owner, pl.ds(piece * PIECE, PIECE)]
    return pltpu.make_async_remote_copy(
        src_ref=part,
        dst_ref=part,
        send_sem=send.at[lane, piece],
        recv_sem=recv.at[lane, piece],
        device_id=target,
        device_id_type=MESH,
    )


def gather_copy(buf, piece, lane, send, recv):
    s, c = place()
    across, beside = lax.rem(c + 2, 4), c + 1 - 2 * lax.rem(c, 2)
    owner = across if lane == 2 else c
    target = across if lane == 0 else beside
    return chan_copy(buf, owner, piece, lane, send, recv, (s, target))


def gather_start(buf, piece, send, recv):
    gather_copy(buf, piece, 0, send, recv).start()
    gather_copy(buf, piece, 1, send, recv).start()


def gather_forward(buf, piece, send, recv):
    gather_copy(buf, piece, 0, send, recv).wait_recv()
    gather_copy(buf, piece, 2, send, recv).start()


def gather_finish(buf, piece, send, recv):
    gather_copy(buf, piece, 1, send, recv).wait()
    gather_copy(buf, piece, 2, send, recv).wait()
    gather_copy(buf, piece, 0, send, recv).wait_send()


def spread_two(f2):
    shape = (ROWS, ROWS)
    row = lax.broadcasted_iota(jnp.int32, shape, 0)
    col = lax.broadcasted_iota(jnp.int32, shape, 1)
    same = jnp.bitwise_and(row, 7) == jnp.bitwise_and(col, 7)
    order = col == jnp.bitwise_and(row, 7) * 64 + lax.shift_right_logical(row, 3)
    order = order.astype(jnp.float32).astype(jnp.bfloat16)
    short = (64, ROWS)
    row = lax.broadcasted_iota(jnp.int32, short, 0)
    col = lax.broadcasted_iota(jnp.int32, short, 1)
    widen = (row == lax.shift_right_logical(col, 3)).astype(jnp.float32).astype(jnp.bfloat16)
    wide = dot(f2.reshape(ROWS, 64), widen).astype(jnp.bfloat16)
    return jnp.where(same, dot(order, wide), 0.0).astype(jnp.bfloat16)


def mixer(
    x, og, f1, f2, scale, shift,
    wm, cot, first_cols, seqmix,
    src, xin, big_two, swap_send, swap_recv, gs, gr, hs, hr,
):
    s, c = place()
    lane = pl.ds(0, 256)
    lane2 = pl.ds(256, 256)
    f32 = jnp.float32
    cot[c] = interleaved(og[lane].astype(f32), og[lane2].astype(f32)).astype(jnp.bfloat16)
    src[0] = interleaved(dot(f1[0], x[lane]), dot(f1[1], x[lane2])).astype(jnp.bfloat16)
    greet()
    swap_start(src.at[0], first_cols, swap_send.at[0], swap_recv.at[0])
    for piece in range(PIECES):
        gather_start(cot, piece, hs, hr)
    xin[...] = interleaved(x[lane].astype(f32), x[lane2].astype(f32)).astype(jnp.bfloat16)
    big_two[...] = spread_two(f2[...])
    swap_wait(src.at[0], first_cols, swap_send.at[0], swap_recv.at[0])
    src[1] = dot(big_two[...], first_cols[...]).astype(jnp.bfloat16)
    swap_start(src.at[1], seqmix, swap_send.at[1], swap_recv.at[1])
    for piece in range(PIECES):
        gather_forward(cot, piece, hs, hr)
    swap_wait(src.at[1], seqmix, swap_send.at[1], swap_recv.at[1])
    for piece in range(PIECES):
        rows = pl.ds(piece * PIECE, PIECE)
        xf = xin[rows].astype(f32)
        opening = jax.nn.sigmoid(xf * scale[...] + shift[...])
        wm[c, rows] = (xf + opening * seqmix[rows].astype(f32)).astype(jnp.bfloat16)
        gather_start(wm, piece, gs, gr)
    for piece in range(PIECES):
        gather_finish(cot, piece, hs, hr)
    for piece in range(PIECES):
        gather_forward(wm, piece, gs, gr)
    for piece in range(PIECES):
        gather_finish(wm, piece, gs, gr)


def call_mixer(layer_in, out_grad, factor_one, factor_two, scale, shift):
    vmem = pl.BlockSpec(memory_space=pltpu.VMEM)
    bf = jnp.bfloat16
    square = jax.ShapeDtypeStruct((ROWS, ROWS), bf)
    whole = jax.ShapeDtypeStruct((4, ROWS, ROWS), bf)
    dma = pltpu.SemaphoreType.DMA
    return pl.pallas_call(
        mixer,
        out_shape=(whole, whole, square, square),
        in_specs=[vmem] * 6,
        out_specs=(vmem,) * 4,
        scratch_shapes=[
            pltpu.VMEM((2, ROWS, ROWS), bf),
            pltpu.VMEM((ROWS, ROWS), bf),
            pltpu.VMEM((ROWS, ROWS), bf),
            dma((2,)),
            dma((2,)),
            dma((3, PIECES)),
            dma((3, PIECES)),
            dma((3, PIECES)),
            dma((3, PIECES)),
        ],
        compiler_params=pltpu.CompilerParams(
            collective_id=0, has_side_effects=True, vmem_limit_bytes=48 << 20
        ),
        name="mixer",
    )(layer_in, out_grad, factor_one, factor_two, scale.reshape(1, -1), shift.reshape(1, -1))


def plain(array):
    width = array.shape[-1]
    return array.reshape(PARTS, 2, 8, width).swapaxes(0, 1).reshape(ROWS, width)


def on_device(
    layer_in,
    factor_one,
    factor_two,
    gate_scale,
    gate_shift,
    norm_gain,
    w_gate,
    w_up,
    w_down,
    out_grad,
):
    rows, width = layer_in.shape
    chan_count = lax.axis_size("chan")
    block_count = factor_one.shape[0]
    block = factor_one.shape[1]
    full_width = width * chan_count
    dims_first = (((0,), (0,)), ((), ()))
    in_float = layer_in.astype(jnp.float32)
    in_blocks = layer_in.reshape(block_count, block, width)
    whole, cot_whole, first_cols, second_rows = call_mixer(
        layer_in, out_grad, factor_one, factor_two, gate_scale, gate_shift
    )
    own = lax.axis_index("chan")
    first_cols = first_cols.reshape(64, 8, width)
    mixed_float = plain(lax.dynamic_index_in_dim(whole, own, 0, False)).astype(jnp.float32)
    whole, cot_whole = [
        jnp.concatenate([plain(part[k]) for k in range(4)], axis=1) for part in (whole, cot_whole)
    ]
    seqmix = plain(second_rows).astype(jnp.float32)
    opening = jax.nn.sigmoid(in_float * gate_scale + gate_shift)
    whole_float = whole.astype(jnp.float32)
    inv_rms = lax.rsqrt(jnp.mean(whole_float * whole_float, axis=1, keepdims=True) + 1e-05)
    normed = (whole_float * inv_rms * norm_gain).astype(jnp.bfloat16)
    gate_pre = jnp.dot(normed, w_gate, preferred_element_type=jnp.float32)
    up_pre = jnp.dot(normed, w_up, preferred_element_type=jnp.float32)
    gate_sigmoid = jax.nn.sigmoid(gate_pre)
    hidden = (gate_pre * gate_sigmoid * up_pre).astype(jnp.bfloat16)
    mlp_cols = lax.psum_scatter(
        lax.dot_general(
            w_down, hidden, (((0,), (1,)), ((), ())), preferred_element_type=jnp.float32
        ).astype(jnp.bfloat16),
        "chan",
        scatter_dimension=0,
        tiled=True,
    ).astype(jnp.float32)
    layer_out = (mixed_float + mlp_cols.T).astype(jnp.bfloat16)
    offset = lax.axis_index("chan") * width
    gain_own = lax.dynamic_slice_in_dim(norm_gain, offset, width, 0)
    hidden_grad = lax.dot_general(
        cot_whole, w_down, (((1,), (1,)), ((), ())), preferred_element_type=jnp.float32
    )
    gate_back = (
        hidden_grad * up_pre * gate_sigmoid * (1.0 + gate_pre * (1.0 - gate_sigmoid))
    ).astype(jnp.bfloat16)
    up_back = (hidden_grad * gate_pre * gate_sigmoid).astype(jnp.bfloat16)
    hidden_width = gate_back.shape[1]
    gate_term = lax.dot_general(normed, gate_back, dims_first, preferred_element_type=jnp.float32)
    up_term = lax.dot_general(normed, up_back, dims_first, preferred_element_type=jnp.float32)
    joint_part = lax.psum_scatter(
        jnp.concatenate(
            [
                jnp.concatenate([gate_term, up_term], axis=1),
                lax.dot_general(cot_whole, hidden, dims_first, preferred_element_type=jnp.float32),
            ],
            axis=1,
        ).astype(jnp.bfloat16),
        "seq",
        scatter_dimension=0,
        tiled=True,
    ).astype(jnp.float32)
    gate_part = joint_part[:, :hidden_width]
    up_part = joint_part[:, hidden_width : 2 * hidden_width]
    down_part = joint_part[:, 2 * hidden_width :]
    contract = (((1,), (1,)), ((), ()))
    total = lax.dot_general(w_gate, gate_back, contract, preferred_element_type=jnp.float32)
    normed_grad = lax.psum_scatter(
        total + lax.dot_general(w_up, up_back, contract, preferred_element_type=jnp.float32),
        "chan",
        scatter_dimension=0,
        tiled=True,
    ).T
    row_local = jnp.sum(normed_grad * gain_own * mixed_float, axis=1, keepdims=True)
    row_dots = lax.psum(row_local, "chan")
    mixed_grad = out_grad.astype(jnp.float32) + inv_rms * gain_own * normed_grad
    mixed_grad = mixed_grad - mixed_float * inv_rms * inv_rms * inv_rms * row_dots / full_width
    gain_local = jnp.sum(normed_grad * mixed_float * inv_rms, axis=0)
    seqmix_grad = (mixed_grad * opening).astype(jnp.bfloat16)
    pre_grad = mixed_grad * seqmix * opening * (1.0 - opening)
    scale_local = jnp.sum(pre_grad * in_float, axis=0)
    shift_local = jnp.sum(pre_grad, axis=0)
    grad_cols = lax.all_to_all(
        seqmix_grad.reshape(block_count, block, width),
        "seq",
        split_axis=1,
        concat_axis=0,
        tiled=True,
    )
    first_grad_cols = jnp.einsum(
        "qjp,jqc->pqc", factor_two, grad_cols, preferred_element_type=jnp.float32
    ).astype(jnp.bfloat16)
    two_local = jnp.einsum(
        "jqc,pqc->qjp", grad_cols, first_cols, preferred_element_type=jnp.float32
    )
    first_grad_rows = lax.all_to_all(
        first_grad_cols, "seq", split_axis=0, concat_axis=1, tiled=True
    )
    input_part = jnp.einsum(
        "pkq,pkc->pqc", factor_one, first_grad_rows, preferred_element_type=jnp.float32
    ).reshape(rows, width)
    one_local = jnp.einsum(
        "pkc,pqc->pkq", first_grad_rows, in_blocks, preferred_element_type=jnp.float32
    )
    one_grad, two_grad = (
        lax.psum(one_local.astype(jnp.bfloat16), "chan").astype(jnp.float32),
        lax.psum(two_local.astype(jnp.bfloat16), "chan").astype(jnp.float32),
    )
    scale_grad, shift_grad, gain_grad = lax.psum((scale_local, shift_local, gain_local), "seq")
    input_grad = (mixed_grad + pre_grad * gate_scale + input_part).astype(jnp.bfloat16)
    return (
        layer_out,
        input_grad,
        one_grad,
        two_grad,
        scale_grad,
        shift_grad,
        gain_grad,
        gate_part,
        up_part,
        down_part.T,
    )


def solution(mesh):
    return jax.shard_map(
        on_device,
        mesh=mesh,
        in_specs=(
            P("seq", "chan"),
            P("seq", None, None),
            P("seq", None, None),
            P("chan"),
            P("chan"),
            P(),
            P(None, "chan"),
            P(None, "chan"),
            P("chan", None),
            P("seq", "chan"),
        ),
        out_specs=(
            P("seq", "chan"),
            P("seq", "chan"),
            P("seq", None, None),
            P("seq", None, None),
            P("chan"),
            P("chan"),
            P("chan"),
            P("seq", "chan"),
            P("seq", "chan"),
            P("chan", "seq"),
        ),
        check_vma=False,
    )
```

```python
import jax
import jax.numpy as jnp
from jax import lax
from jax.experimental import pallas as pl
from jax.experimental.pallas import tpu as pltpu
from jax.sharding import PartitionSpec as P

MESH = pl.DeviceIdType.MESH
PARTS = 32
SLAB = 16
ROWS = 512
PIECES = 4
PIECE = ROWS // PIECES
BLOCK = 512
HIDDEN = 1024
UNITS = 6
SLOTS = 4
SHARE = 64
VMEM_LIMIT = 67000000


def interleaved(low, high):
    rows, width = low.shape
    pair = [part.reshape(rows // 8, 8, width) for part in (low, high)]
    return jnp.stack(pair, axis=1).reshape(2 * rows, width)


def inside(ref, piece):
    return interleaved(
        *[full(ref[pl.ds(k * 256 + piece * PIECE // 2, PIECE // 2)]) for k in range(2)]
    )


def deal(whole):
    parts = whole.reshape(PARTS, 2, 8, whole.shape[1])
    return [parts[:, k].reshape(ROWS // 2, whole.shape[1]) for k in range(2)]


def dot(a, b):
    return jnp.dot(a, b, preferred_element_type=jnp.float32)


def dot_rows(a, b):
    return lax.dot_general(a, b, (((1,), (1,)), ((), ())), preferred_element_type=jnp.float32)


def half(values):
    return values.astype(jnp.bfloat16)


def full(values):
    return values.astype(jnp.float32)


def place():
    return lax.axis_index("seq"), lax.axis_index("chan")


def greet():
    s, c = place()
    barrier = pltpu.get_barrier_semaphore()

    def greet_seq(step, carry):
        target = (lax.rem(s + step, PARTS), c)
        pl.semaphore_signal(barrier, inc=1, device_id=target, device_id_type=MESH)
        return carry

    lax.fori_loop(1, PARTS, greet_seq, 0)
    for step in range(1, 4):
        target = (s, lax.rem(c + step, 4))
        pl.semaphore_signal(barrier, inc=1, device_id=target, device_id_type=MESH)
    pl.semaphore_wait(barrier, PARTS - 1 + 3)


def slab(index):
    return pl.ds(pl.multiple_of(index * SLAB, SLAB), SLAB)


def swap_start(src, dst, send, recv):
    s, c = place()

    def one(step, carry):
        target = lax.rem(s + step, PARTS)
        pltpu.make_async_remote_copy(
            src_ref=src.at[slab(target)],
            dst_ref=dst.at[slab(s)],
            send_sem=send,
            recv_sem=recv,
            device_id=(target, c),
            device_id_type=MESH,
        ).start()
        return carry

    lax.fori_loop(1, PARTS, one, 0)
    dst[slab(s), :] = src[slab(s), :]


def swap_wait(src, dst, send, recv):
    s, c = place()
    most = pl.ds(0, ROWS - SLAB)
    pltpu.make_async_remote_copy(
        src_ref=src.at[most],
        dst_ref=dst.at[most],
        send_sem=send,
        recv_sem=recv,
        device_id=(lax.rem(s + 1, PARTS), c),
        device_id_type=MESH,
    ).wait()


def chan_copy(buf, owner, piece, lane, send, recv, target):
    part = buf.at[owner, pl.ds(piece * PIECE, PIECE)]
    return pltpu.make_async_remote_copy(
        src_ref=part,
        dst_ref=part,
        send_sem=send.at[lane, piece],
        recv_sem=recv.at[lane, piece],
        device_id=target,
        device_id_type=MESH,
    )


def gather_copy(buf, piece, lane, send, recv):
    s, c = place()
    across, beside = lax.rem(c + 2, 4), c + 1 - 2 * lax.rem(c, 2)
    owner = across if lane == 2 else c
    target = across if lane == 0 else beside
    return chan_copy(buf, owner, piece, lane, send, recv, (s, target))


def gather_start(buf, piece, send, recv):
    gather_copy(buf, piece, 0, send, recv).start()
    gather_copy(buf, piece, 1, send, recv).start()


def gather_forward(buf, piece, send, recv):
    gather_copy(buf, piece, 0, send, recv).wait_recv()
    gather_copy(buf, piece, 2, send, recv).start()


def gather_finish(buf, piece, send, recv):
    gather_copy(buf, piece, 1, send, recv).wait()
    gather_copy(buf, piece, 2, send, recv).wait()
    gather_copy(buf, piece, 0, send, recv).wait_send()


def bits(mask):
    return half(mask.astype(jnp.float32))


def index_pair(shape):
    return lax.broadcasted_iota(jnp.int32, shape, 0), lax.broadcasted_iota(jnp.int32, shape, 1)


def same_place():
    row, col = index_pair((ROWS, ROWS))
    return jnp.bitwise_and(row, 7) == jnp.bitwise_and(col, 7)


def reorder(transposed):
    row, col = index_pair((ROWS, ROWS))
    if transposed:
        row, col = col, row
    return bits(col == jnp.bitwise_and(row, 7) * 64 + lax.shift_right_logical(row, 3))


def widen():
    row, col = index_pair((64, ROWS))
    return bits(row == lax.shift_right_logical(col, 3))


def spread_two(f2):
    wide = half(dot(f2.reshape(ROWS, 64), widen()))
    return half(jnp.where(same_place(), dot(reorder(False), wide), 0.0))


def gather_two(product):
    tall = half(dot_rows(half(jnp.where(same_place(), product, 0.0)), widen()))
    return half(dot(reorder(True), tall))


def remote(src, dst, send, recv, target):
    return pltpu.make_async_remote_copy(
        src_ref=src, dst_ref=dst, send_sem=send, recv_sem=recv,
        device_id=target, device_id_type=MESH,
    )


def axis_place(axis):
    s, _ = place()
    return lax.rem(s, 4) if axis == 0 else lax.div(s, 8)


def axis_peer(axis, step):
    s, c = place()
    here = axis_place(axis)
    there = lax.rem(here + step, 4)
    return s + (there - here) * (1 if axis == 0 else 8), c


class Ring:
    def __init__(self, view, early, late, send, recv, axis):
        self.view, self.early, self.late = view, early, late
        self.send, self.recv = send, recv
        self.here = axis_place(axis)
        self.ahead, self.behind = axis_peer(axis, 1), axis_peer(axis, 3)

    def copy(self, index):
        after, across, before = [lax.rem(self.here + k, 4) for k in (1, 2, 3)]
        src, dst, target = (
            lambda: (self.view(0, across), self.early.at[0], self.ahead),
            lambda: (self.view(1, across), self.early.at[1], self.behind),
            lambda: (self.view(1, after), self.late.at[0, 1], self.ahead),
            lambda: (self.view(0, before), self.late.at[1, 0], self.behind),
            lambda: (self.view(0, after), self.late.at[0, 0], self.ahead),
            lambda: (self.view(1, before), self.late.at[1, 1], self.behind),
        )[index]()
        return remote(src, dst, self.send.at[index], self.recv.at[index], target)

    def start(self):
        for index in range(4):
            self.copy(index).start()

    def middle(self):
        after, before = lax.rem(self.here + 1, 4), lax.rem(self.here + 3, 4)
        for way, owner in ((0, after), (1, before)):
            self.copy(way).wait_recv()
            mine = self.view(way, owner)
            mine[...] = half(full(mine[...]) + full(self.early[way]))
            self.copy(4 + way).start()

    def arrive(self):
        for index in range(2, 6):
            self.copy(index).wait_recv()

    def total(self, part):
        return full(self.view(part, self.here)[...]) + (
            full(self.late[0, part]) + full(self.late[1, part])
        )

    def settle(self):
        for index in range(6):
            self.copy(index).wait_send()


class Grads:
    def __init__(self, own, bufs, sems, result):
        self.own, self.result = own, result
        self.early_one, self.late_one, self.early_two, self.late_two, self.last = bufs
        self.send, self.recv = sems

    def ring(self, unit, stage):
        slot, first = unit % SLOTS, unit % 2
        sems = [s.at[unit, stage] for s in (self.send, self.recv)]
        if stage == 0:
            view = lambda part, owner: self.own.at[slot, part, owner]
            return Ring(view, self.early_one.at[unit], self.late_one.at[unit], *sems, first)
        here = axis_place(first)
        view = lambda part, owner: self.own.at[slot, part, here, owner]
        return Ring(view, self.early_two.at[unit], self.late_two.at[unit], *sems, 1 - first)

    def multiply(self, unit, left, right):
        slot = unit % SLOTS
        own = self.own
        if unit >= SLOTS:
            self.last_copy(unit - SLOTS).wait_send()

        @pl.loop(0, 4)
        def _(z):
            rows = pl.ds(pl.multiple_of(z * 512, 512), 512)
            tile = half(dot(left[rows, :], right).reshape(2, 4, SHARE, BLOCK))
            if unit % 2 == 0:
                own[slot, :, :, z] = tile
            else:
                own[slot, :, z] = tile

        self.ring(unit, 0).start()

    def middle(self, unit, stage):
        self.ring(unit, stage).middle()

    def turn(self, unit):
        ring = self.ring(unit, 0)
        ring.arrive()

        @pl.loop(0, 2)
        def _(part):
            ring.view(part, ring.here)[...] = half(ring.total(part))

        self.ring(unit, 1).start()
        ring.settle()

    def last_copy(self, unit):
        s, c = place()
        near = lax.rem(lax.div(s, 4), 2)
        ring = self.ring(unit, 1)
        sems = [s.at[unit, 2, 0] for s in (self.send, self.recv)]
        src = ring.view(1 - near, ring.here)
        return remote(src, self.last.at[unit], *sems, (s + 4 - 8 * near, c))

    def finish(self, unit):
        s, _ = place()
        near = lax.rem(lax.div(s, 4), 2)
        ring = self.ring(unit, 1)
        ring.arrive()
        ring.view(1 - near, ring.here)[...] = half(ring.total(1 - near))
        self.last_copy(unit).start()
        self.result[unit // 2, :, pl.ds(unit % 2 * BLOCK, BLOCK)] = ring.total(near)
        ring.settle()

    def close(self, unit):
        self.last_copy(unit).wait_recv()
        if unit + SLOTS >= UNITS:
            self.last_copy(unit).wait_send()
        cols = pl.ds(unit % 2 * BLOCK, BLOCK)
        self.result[unit // 2, :, cols] = self.result[unit // 2, :, cols] + full(self.last[unit])


class ChanSum:
    def __init__(self, part, near, far, send, recv):
        self.part, self.near, self.far, self.send, self.recv = part, near, far, send, recv
        s, c = place()
        self.high, self.core = lax.div(c, 2), lax.rem(c, 2)
        self.beside, self.across = (s, c + 1 - 2 * self.core), (s, lax.rem(c + 2, 4))

    def near_copy(self, high):
        return remote(
            self.part.at[high * 2 + 1 - self.core], self.near.at[high],
            self.send.at[high], self.recv.at[high], self.beside,
        )

    def far_copy(self):
        return remote(
            self.part.at[(1 - self.high) * 2 + self.core], self.far,
            self.send.at[2], self.recv.at[2], self.across,
        )

    def start(self):
        for high in range(2):
            self.near_copy(high).start()

    def onward(self):
        for high in range(2):
            self.near_copy(high).wait()
        other = 1 - self.high
        slot = other * 2 + self.core
        self.part[slot] = half(full(self.part[slot]) + full(self.near[other]))
        self.far_copy().start()

    def arrive(self):
        self.far_copy().wait()

    def total(self, rows):
        mine = full(self.part[self.high * 2 + self.core, rows])
        return mine + full(self.near[self.high, rows]) + full(self.far[rows])


class PairSum:
    def __init__(self, part, got, send, recv):
        self.part, self.got, self.send, self.recv = part, got, send, recv
        s, c = place()
        self.targets = (s, c + 1 - 2 * lax.rem(c, 2)), (s, lax.rem(c + 2, 4))

    def copy(self, step):
        return remote(
            self.part.at[step], self.got.at[step],
            self.send.at[step], self.recv.at[step], self.targets[step],
        )

    def start(self, values):
        self.part[0] = values
        self.copy(0).start()

    def onward(self):
        self.copy(0).wait()
        self.part[1] = half(full(self.part[0]) + full(self.got[0]))
        self.copy(1).start()

    def finish(self):
        self.copy(1).wait()
        return full(self.part[1]) + full(self.got[1])


class SeqSum:
    def __init__(self, slots, send, recv):
        self.slots, self.send, self.recv = slots, send, recv

    def copy(self, axis, step):
        mine = self.slots.at[axis, axis_place(axis)]
        return remote(
            mine, mine, self.send.at[axis, step], self.recv.at[axis, step],
            axis_peer(axis, step),
        )

    def pair_copy(self):
        s, c = place()
        near = lax.rem(lax.div(s, 4), 2)
        mine = self.slots.at[2, near]
        return remote(
            mine, mine, self.send.at[2, 1], self.recv.at[2, 1], (s + 4 - 8 * near, c)
        )

    def start(self, values):
        self.slots[0, axis_place(0)] = values
        for step in range(1, 4):
            self.copy(0, step).start()

    def take(self, axis):
        for step in range(1, 4):
            self.copy(axis, step).wait()
        return (self.slots[axis, 0] + self.slots[axis, 1]) + (
            self.slots[axis, 2] + self.slots[axis, 3]
        )

    def second(self):
        self.slots[1, axis_place(1)] = self.take(0)
        for step in range(1, 4):
            self.copy(1, step).start()

    def third(self):
        s, _ = place()
        self.slots[2, lax.rem(lax.div(s, 4), 2)] = self.take(1)
        self.pair_copy().start()

    def finish(self):
        self.pair_copy().wait()
        return self.slots[2, 0] + self.slots[2, 1]


def layer(
    x, og, f1, f2, scale, shift, gain, wg_hbm, wu_hbm, wd_hbm,
    layer_out, input_grad, one_grad, two_grad, vectors, grads_out,
    wg, wu, wd, cot, flipped, wm, normed, gate_pre, up_pre, hidden, gate_back, up_back,
    inv, dots, first_cols, seqmix, back_cols, first_back, src, big_two,
    sum_near, sum_far, own, early_one, late_one, early_two, late_two, last,
    one_part, one_got, two_part, two_got, slots,
    w_sem, swap_send, swap_recv, gs, gr, hs, hr, grad_send, grad_recv, sum_send, sum_recv,
    dot_send, dot_recv, pair_send, pair_recv, vec_send, vec_recv,
):
    s, c = place()
    top, low = pl.ds(0, 256), pl.ds(256, 256)
    swap = lambda k: (swap_send.at[k], swap_recv.at[k])
    weights = [
        pltpu.make_async_copy(a, b, w_sem.at[k])
        for k, (a, b) in enumerate(((wg_hbm, wg), (wu_hbm, wu), (wd_hbm, wd)))
    ]
    for copy in weights:
        copy.start()
    for piece in range(PIECES):
        cot[c, pl.ds(piece * PIECE, PIECE)] = half(inside(og, piece))
    src[0] = half(interleaved(dot(f1[0], x[top]), dot(f1[1], x[low])))
    greet()
    swap_start(src.at[0], first_cols, *swap(0))
    for piece in range(PIECES):
        gather_start(cot, piece, hs, hr)
    big_two[0] = spread_two(f2[...])
    big_two[1] = big_two[0].T
    swap_wait(src.at[0], first_cols, *swap(0))
    src[1] = half(dot(big_two[0], first_cols[...]))
    swap_start(src.at[1], seqmix, *swap(1))
    for piece in range(PIECES):
        gather_forward(cot, piece, hs, hr)
    swap_wait(src.at[1], seqmix, *swap(1))
    for piece in range(PIECES):
        rows = pl.ds(piece * PIECE, PIECE)
        xf = inside(x, piece)
        opening = jax.nn.sigmoid(xf * scale[...] + shift[...])
        wm[c, rows] = half(xf + opening * full(seqmix[rows]))
        gather_start(wm, piece, gs, gr)
    for piece in range(PIECES):
        gather_finish(cot, piece, hs, hr)
    for k in range(4):
        flipped[pl.ds(k * BLOCK, BLOCK), :] = cot[k].T
    for piece in range(PIECES):
        gather_forward(wm, piece, gs, gr)
    for copy in weights:
        copy.wait()

    for part in range(2):
        for piece in (2 * part, 2 * part + 1):
            gather_finish(wm, piece, gs, gr)

        @pl.loop(0, 4)
        def _(k):
            rows = pl.ds(pl.multiple_of(part * 256 + k * 64, 64), 64)
            blocks = [full(wm[chan, rows]) for chan in range(4)]
            squares = sum(jnp.sum(b * b, axis=1, keepdims=True) for b in blocks)
            scaled = lax.rsqrt(squares / (4 * BLOCK) + 1e-05)
            inv[rows] = jnp.broadcast_to(scaled, (64, 128))
            for chan in range(4):
                normed[chan, rows] = half(blocks[chan] * scaled * gain[chan])

        rows = pl.ds(part * 256, 256)
        for k in range(2):
            cols = pl.ds(k * BLOCK, BLOCK)
            gate = up = 0.0
            for chan in range(4):
                deep = pl.ds(chan * BLOCK, BLOCK)
                gate = gate + dot(normed[chan, rows], wg[deep, cols])
                up = up + dot(normed[chan, rows], wu[deep, cols])
            gate_pre[rows, cols] = gate
            up_pre[rows, cols] = up
            hidden[rows, cols] = half(gate * jax.nn.sigmoid(gate) * up)

    grads = Grads(
        own, (early_one, late_one, early_two, late_two, last), (grad_send, grad_recv), grads_out
    )
    lows, highs = pl.ds(0, BLOCK), pl.ds(BLOCK, BLOCK)
    grads.multiply(0, flipped, hidden[:, lows])
    grads.multiply(1, flipped, hidden[:, highs])
    for k in range(4):
        flipped[pl.ds(k * BLOCK, BLOCK), :] = normed[k].T

    for part in range(2):
        rows = pl.ds(part * 256, 256)
        products = 0.0
        for k in range(2):
            cols = pl.ds(k * BLOCK, BLOCK)
            hidden_grad = 0.0
            for chan in range(4):
                deep = pl.ds(chan * BLOCK, BLOCK)
                hidden_grad = hidden_grad + dot_rows(cot[chan, rows], wd[cols, deep])
            gate, up = gate_pre[rows, cols], up_pre[rows, cols]
            s_gate = jax.nn.sigmoid(gate)
            back = half(hidden_grad * up * s_gate * (1.0 + gate * (1.0 - s_gate)))
            gate_back[rows, cols] = back
            products = products + jnp.sum(full(back) * gate, axis=1, keepdims=True)
            back = half(hidden_grad * gate * s_gate)
            up_back[rows, cols] = back
            products = products + jnp.sum(full(back) * up, axis=1, keepdims=True)
        turned = jnp.broadcast_to(products, (256, 128)).T
        dots[c, :, rows] = turned[:8]
    dot_copies = [
        remote(dots.at[c], dots.at[c], dot_send.at[k], dot_recv.at[k], (s, lax.rem(c + k, 4)))
        for k in range(1, 4)
    ]
    for copy in dot_copies:
        copy.start()

    def joint_back(chan):
        rows = pl.ds(pl.multiple_of(chan * BLOCK, BLOCK), BLOCK)
        return half(dot_rows(gate_back[...], wg[rows, :]) + dot_rows(up_back[...], wu[rows, :]))

    @pl.loop(0, 4)
    def _(chan):
        normed[chan] = joint_back(chan)

    back_sum = ChanSum(
        normed, sum_near.at[0], sum_far.at[0], sum_send.at[0], sum_recv.at[0]
    )
    back_sum.start()
    grads.middle(0, 0)
    grads.middle(1, 0)
    grads.multiply(2, flipped, gate_back[:, lows])
    grads.multiply(3, flipped, gate_back[:, highs])
    back_sum.onward()

    for chan in range(4):
        cols = pl.ds(chan * BLOCK, BLOCK)
        cot[chan] = half(dot(hidden[...], wd[:, cols]))
    out_sum = ChanSum(cot, sum_near.at[1], sum_far.at[1], sum_send.at[1], sum_recv.at[1])
    out_sum.start()
    grads.turn(0)
    grads.turn(1)
    out_sum.onward()
    grads.middle(2, 0)
    grads.middle(3, 0)
    for copy in dot_copies:
        copy.wait()
    row_total = (dots[0] + dots[1]) + (dots[2] + dots[3])
    up_pre[:, pl.ds(0, 128)] = jnp.broadcast_to(row_total[:1], (128, ROWS)).T
    grads.middle(0, 1)
    grads.middle(1, 1)

    back_sum.arrive()
    sums = [0.0, 0.0, 0.0]
    for piece in range(PIECES):
        rows = pl.ds(piece * PIECE, PIECE)
        normed_grad = back_sum.total(rows)
        scaled, total = inv[rows][:, :1], up_pre[rows, pl.ds(0, 128)][:, :1]
        mixed, xf = full(wm[c, rows]), inside(x, piece)
        mixed_grad = inside(og, piece) + scaled * gain[c] * normed_grad
        mixed_grad = mixed_grad - mixed * (scaled * scaled * total / (4 * BLOCK))
        opening = jax.nn.sigmoid(xf * scale[...] + shift[...])
        src[0, rows] = half(mixed_grad * opening)
        pre_grad = mixed_grad * full(seqmix[rows]) * opening * (1.0 - opening)
        gate_pre[rows, lows] = mixed_grad + pre_grad * scale[...]
        for k, term in enumerate((pre_grad * xf, pre_grad, normed_grad * mixed * scaled)):
            sums[k] = sums[k] + jnp.sum(term, axis=0, keepdims=True)
    swap_start(src.at[0], back_cols, *swap(2))
    vector_sum = SeqSum(slots, vec_send, vec_recv)
    row, _ = index_pair((8, BLOCK))
    vector_sum.start(
        jnp.where(row == 0, sums[0], jnp.where(row == 1, sums[1], jnp.where(row == 2, sums[2], 0.0)))
    )
    grads.finish(0)
    grads.finish(1)
    grads.multiply(4, flipped, up_back[:, lows])
    grads.multiply(5, flipped, up_back[:, highs])
    swap_wait(src.at[0], back_cols, *swap(2))
    src[1] = half(dot(big_two[1], back_cols[...]))
    swap_start(src.at[1], first_back, *swap(3))
    vector_sum.second()
    two_sum = PairSum(two_part, two_got, pair_send.at[0], pair_recv.at[0])
    two_sum.start(gather_two(dot_rows(back_cols[...], first_cols[...])))
    grads.turn(2)
    grads.turn(3)
    grads.middle(4, 0)
    grads.middle(5, 0)
    two_sum.onward()
    vector_sum.third()
    out_sum.arrive()
    plain_out = deal(full(wm[c]) + out_sum.total(pl.ds(0, ROWS)))
    layer_out[top] = half(plain_out[0])
    layer_out[low] = half(plain_out[1])
    grads.middle(2, 1)
    grads.middle(3, 1)
    swap_wait(src.at[1], first_back, *swap(3))
    one_sum = PairSum(one_part, one_got, pair_send.at[1], pair_recv.at[1])
    blocks = [half(b) for b in deal(full(first_back[...]))]
    one_sum.start(
        jnp.concatenate(
            [half(dot_rows(blocks[0], x[top])), half(dot_rows(blocks[1], x[low]))], axis=0
        )
    )
    kept_plain = deal(gate_pre[:, lows])
    for k, rows in enumerate((top, low)):
        input_grad[rows] = half(kept_plain[k] + dot(f1[k].T, blocks[k]))
    grads.finish(2)
    grads.finish(3)
    one_sum.onward()
    two_grad[...] = two_sum.finish()
    vectors[...] = vector_sum.finish()
    grads.turn(4)
    grads.turn(5)
    grads.middle(4, 1)
    grads.middle(5, 1)
    one_grad[...] = one_sum.finish()
    for unit in range(4):
        grads.close(unit)
    grads.finish(4)
    grads.finish(5)
    grads.close(4)
    grads.close(5)


def on_device(
    layer_in, factor_one, factor_two, gate_scale, gate_shift, norm_gain, w_gate, w_up, w_down, out_grad
):
    vmem, away = pl.BlockSpec(memory_space=pltpu.VMEM), pl.BlockSpec(memory_space=pl.ANY)
    bf, f32 = jnp.bfloat16, jnp.float32
    dma = pltpu.SemaphoreType.DMA
    square = pltpu.VMEM((ROWS, BLOCK), bf)
    whole = pltpu.VMEM((4, ROWS, BLOCK), bf)
    flipped = pltpu.VMEM((4 * BLOCK, ROWS), bf)
    wide = pltpu.VMEM((ROWS, HIDDEN), bf)
    wide_float = pltpu.VMEM((ROWS, HIDDEN), f32)
    out = jax.ShapeDtypeStruct
    outs = pl.pallas_call(
        layer,
        out_shape=(
            out((ROWS, BLOCK), bf),
            out((ROWS, BLOCK), bf),
            out((2 * 256, 256), f32),
            out((ROWS, 64), f32),
            out((8, BLOCK), f32),
            out((3, SHARE, HIDDEN), f32),
        ),
        in_specs=[vmem] * 7 + [away] * 3,
        out_specs=(vmem,) * 6,
        scratch_shapes=[
            pltpu.VMEM((4 * BLOCK, HIDDEN), bf),
            pltpu.VMEM((4 * BLOCK, HIDDEN), bf),
            pltpu.VMEM((HIDDEN, 4 * BLOCK), bf),
            whole, flipped, whole, whole,
            wide_float, wide_float, wide, wide, wide,
            pltpu.VMEM((ROWS, 128), f32),
            pltpu.VMEM((4, 8, ROWS), f32),
            square, square, square, square,
            pltpu.VMEM((2, ROWS, BLOCK), bf),
            pltpu.VMEM((2, ROWS, BLOCK), bf),
            pltpu.VMEM((2, 2, ROWS, BLOCK), bf),
            pltpu.VMEM((2, ROWS, BLOCK), bf),
            pltpu.VMEM((SLOTS, 2, 4, 4, SHARE, BLOCK), bf),
            pltpu.VMEM((UNITS, 2, 4, SHARE, BLOCK), bf),
            pltpu.VMEM((UNITS, 2, 2, 4, SHARE, BLOCK), bf),
            pltpu.VMEM((UNITS, 2, SHARE, BLOCK), bf),
            pltpu.VMEM((UNITS, 2, 2, SHARE, BLOCK), bf),
            pltpu.VMEM((UNITS, SHARE, BLOCK), bf),
            pltpu.VMEM((2, 2 * 256, 256), bf),
            pltpu.VMEM((2, 2 * 256, 256), bf),
            pltpu.VMEM((2, ROWS, 64), bf),
            pltpu.VMEM((2, ROWS, 64), bf),
            pltpu.VMEM((3, 4, 8, BLOCK), f32),
            dma((3,)),
            dma((4,)), dma((4,)),
            dma((3, PIECES)), dma((3, PIECES)), dma((3, PIECES)), dma((3, PIECES)),
            dma((UNITS, 3, 6)), dma((UNITS, 3, 6)),
            dma((2, 3)), dma((2, 3)),
            dma((4,)), dma((4,)),
            dma((2, 2)), dma((2, 2)),
            dma((3, 4)), dma((3, 4)),
        ],
        compiler_params=pltpu.CompilerParams(
            collective_id=0, has_side_effects=True, vmem_limit_bytes=VMEM_LIMIT
        ),
        name="layer",
    )(
        layer_in, out_grad, factor_one, factor_two,
        gate_scale.reshape(1, -1), gate_shift.reshape(1, -1), norm_gain.reshape(4, 1, -1),
        w_gate, w_up, w_down,
    )
    layer_out, input_grad, one_grad, two_grad, vectors, grads = outs
    return (
        layer_out,
        input_grad,
        one_grad.reshape(factor_one.shape),
        two_grad.reshape(factor_two.shape),
        vectors[0],
        vectors[1],
        vectors[2],
        grads[1],
        grads[2],
        grads[0].T,
    )


def solution(mesh):
    return jax.shard_map(
        on_device,
        mesh=mesh,
        in_specs=(
            P("seq", "chan"),
            P("seq", None, None),
            P("seq", None, None),
            P("chan"),
            P("chan"),
            P(),
            P(None, "chan"),
            P(None, "chan"),
            P("chan", None),
            P("seq", "chan"),
        ),
        out_specs=(
            P("seq", "chan"),
            P("seq", "chan"),
            P("seq", None, None),
            P("seq", None, None),
            P("chan"),
            P("chan"),
            P("chan"),
            P("seq", "chan"),
            P("seq", "chan"),
            P("chan", "seq"),
        ),
        check_vma=False,
    )
```

```python
import jax
import jax.numpy as jnp
from jax import lax
from jax.experimental import pallas as pl
from jax.experimental.pallas import tpu as pltpu
from jax.sharding import PartitionSpec as P

MESH = pl.DeviceIdType.MESH
PARTS = 32
SLAB = 16
ROWS = 512
PIECES = 4
PIECE = ROWS // PIECES
BLOCK = 512
HIDDEN = 1024
UNITS = 6
SLOTS = 4
SHARE = 64
EARLY = 2
OUTPUTS = 10
VMEM_LIMIT = 67000000


def interleaved(low, high):
    rows, width = low.shape
    pair = [part.reshape(rows // 8, 8, width) for part in (low, high)]
    return jnp.stack(pair, axis=1).reshape(2 * rows, width)


def inside(ref, piece):
    return interleaved(
        *[full(ref[pl.ds(k * 256 + piece * PIECE // 2, PIECE // 2)]) for k in range(2)]
    )


def deal(whole):
    parts = whole.reshape(PARTS, 2, 8, whole.shape[1])
    return [parts[:, k].reshape(ROWS // 2, whole.shape[1]) for k in range(2)]


def dot(a, b):
    return jnp.dot(a, b, preferred_element_type=jnp.float32)


def dot_rows(a, b):
    return lax.dot_general(a, b, (((1,), (1,)), ((), ())), preferred_element_type=jnp.float32)


def half(values):
    return values.astype(jnp.bfloat16)


def full(values):
    return values.astype(jnp.float32)


def place():
    return lax.axis_index("seq"), lax.axis_index("chan")


def greet():
    s, c = place()
    barrier = pltpu.get_barrier_semaphore()

    def greet_seq(step, carry):
        target = (lax.rem(s + step, PARTS), c)
        pl.semaphore_signal(barrier, inc=1, device_id=target, device_id_type=MESH)
        return carry

    lax.fori_loop(1, PARTS, greet_seq, 0)
    for step in range(1, 4):
        target = (s, lax.rem(c + step, 4))
        pl.semaphore_signal(barrier, inc=1, device_id=target, device_id_type=MESH)


def greeted():
    pl.semaphore_wait(pltpu.get_barrier_semaphore(), PARTS - 1 + 3)


def slab(index):
    return pl.ds(pl.multiple_of(index * SLAB, SLAB), SLAB)


def swap_start(src, dst, send, recv):
    s, c = place()

    def one(step, carry):
        target = lax.rem(s + step, PARTS)
        pltpu.make_async_remote_copy(
            src_ref=src.at[slab(target)],
            dst_ref=dst.at[slab(s)],
            send_sem=send,
            recv_sem=recv,
            device_id=(target, c),
            device_id_type=MESH,
        ).start()
        return carry

    lax.fori_loop(1, PARTS, one, 0)
    dst[slab(s), :] = src[slab(s), :]


def swap_wait(src, dst, send, recv):
    s, c = place()
    most = pl.ds(0, ROWS - SLAB)
    pltpu.make_async_remote_copy(
        src_ref=src.at[most],
        dst_ref=dst.at[most],
        send_sem=send,
        recv_sem=recv,
        device_id=(lax.rem(s + 1, PARTS), c),
        device_id_type=MESH,
    ).wait()


def chan_copy(buf, owner, piece, lane, send, recv, target):
    part = buf.at[owner, pl.ds(piece * PIECE, PIECE)]
    return pltpu.make_async_remote_copy(
        src_ref=part,
        dst_ref=part,
        send_sem=send.at[lane, piece],
        recv_sem=recv.at[lane, piece],
        device_id=target,
        device_id_type=MESH,
    )


def gather_copy(buf, piece, lane, send, recv):
    s, c = place()
    across, beside = lax.rem(c + 2, 4), c + 1 - 2 * lax.rem(c, 2)
    owner = across if lane == 2 else c
    target = across if lane == 0 else beside
    return chan_copy(buf, owner, piece, lane, send, recv, (s, target))


def gather_start(buf, piece, send, recv):
    gather_copy(buf, piece, 0, send, recv).start()
    gather_copy(buf, piece, 1, send, recv).start()


def gather_forward(buf, piece, send, recv):
    gather_copy(buf, piece, 0, send, recv).wait_recv()
    gather_copy(buf, piece, 2, send, recv).start()


def gather_finish(buf, piece, send, recv):
    gather_copy(buf, piece, 1, send, recv).wait()
    gather_copy(buf, piece, 2, send, recv).wait()
    gather_copy(buf, piece, 0, send, recv).wait_send()


def bits(mask):
    return half(mask.astype(jnp.float32))


def index_pair(shape):
    return lax.broadcasted_iota(jnp.int32, shape, 0), lax.broadcasted_iota(jnp.int32, shape, 1)


def same_place():
    row, col = index_pair((ROWS, ROWS))
    return jnp.bitwise_and(row, 7) == jnp.bitwise_and(col, 7)


def reorder(transposed):
    row, col = index_pair((ROWS, ROWS))
    if transposed:
        row, col = col, row
    return bits(col == jnp.bitwise_and(row, 7) * 64 + lax.shift_right_logical(row, 3))


def widen():
    row, col = index_pair((64, ROWS))
    return bits(row == lax.shift_right_logical(col, 3))


def spread_two(f2):
    wide = half(dot(f2.reshape(ROWS, 64), widen()))
    return half(jnp.where(same_place(), dot(reorder(False), wide), 0.0))


def gather_two(product):
    tall = half(dot_rows(half(jnp.where(same_place(), product, 0.0)), widen()))
    return half(dot(reorder(True), tall))


def remote(src, dst, send, recv, target):
    return pltpu.make_async_remote_copy(
        src_ref=src, dst_ref=dst, send_sem=send, recv_sem=recv,
        device_id=target, device_id_type=MESH,
    )


def axis_place(axis):
    s, _ = place()
    return lax.rem(s, 4) if axis == 0 else lax.div(s, 8)


def axis_peer(axis, step):
    s, c = place()
    here = axis_place(axis)
    there = lax.rem(here + step, 4)
    return s + (there - here) * (1 if axis == 0 else 8), c


class Ring:
    def __init__(self, view, early, late, send, recv, axis):
        self.view, self.early, self.late = view, early, late
        self.send, self.recv = send, recv
        self.here = axis_place(axis)
        self.ahead, self.behind = axis_peer(axis, 1), axis_peer(axis, 3)

    def copy(self, index):
        after, across, before = [lax.rem(self.here + k, 4) for k in (1, 2, 3)]
        src, dst, target = (
            lambda: (self.view(0, across), self.early.at[0], self.ahead),
            lambda: (self.view(1, across), self.early.at[1], self.behind),
            lambda: (self.view(1, after), self.late.at[0, 1], self.ahead),
            lambda: (self.view(0, before), self.late.at[1, 0], self.behind),
            lambda: (self.view(0, after), self.late.at[0, 0], self.ahead),
            lambda: (self.view(1, before), self.late.at[1, 1], self.behind),
        )[index]()
        return remote(src, dst, self.send.at[index], self.recv.at[index], target)

    def start(self):
        for index in range(4):
            self.copy(index).start()

    def middle(self):
        after, before = lax.rem(self.here + 1, 4), lax.rem(self.here + 3, 4)
        for way, owner in ((0, after), (1, before)):
            self.copy(way).wait_recv()
            mine = self.view(way, owner)
            mine[...] = half(full(mine[...]) + full(self.early[way]))
            self.copy(4 + way).start()

    def arrive(self):
        for index in range(2, 6):
            self.copy(index).wait_recv()

    def total(self, part):
        return full(self.view(part, self.here)[...]) + (
            full(self.late[0, part]) + full(self.late[1, part])
        )

    def settle(self):
        for index in range(6):
            self.copy(index).wait_send()


class Grads:
    def __init__(self, own, mid, bufs, sems, result, out, out_sem):
        self.own, self.mid, self.result = own, mid, result
        self.out, self.out_sem = out, out_sem
        self.early_one, self.late_one, self.early_two, self.late_two, self.last = bufs
        self.send, self.recv = sems

    def ring(self, unit, stage):
        slot, first = unit % SLOTS, unit % 2
        sems = [s.at[unit, stage] for s in (self.send, self.recv)]
        if stage == 0:
            view = lambda part, owner: self.own.at[slot, part, owner]
            return Ring(view, self.early_one.at[unit], self.late_one.at[unit], *sems, first)
        view = lambda part, owner: self.mid.at[slot, part, owner]
        return Ring(view, self.early_two.at[unit], self.late_two.at[unit], *sems, 1 - first)

    def multiply(self, unit, left, right):
        slot = unit % SLOTS
        own = self.own
        for z in range(4):
            tile = half(dot(left[pl.ds(z * 512, 512), :], right).reshape(2, 4, SHARE, BLOCK))
            if unit % 2 == 0:
                own[slot, :, :, z] = tile
            else:
                own[slot, :, z] = tile

        self.ring(unit, 0).start()

    def middle(self, unit, stage):
        self.ring(unit, stage).middle()

    def turn(self, unit):
        ring = self.ring(unit, 0)
        ring.arrive()
        if unit >= SLOTS:
            self.last_copy(unit - SLOTS).wait_send()

        @pl.loop(0, 2)
        def _(part):
            self.mid[unit % SLOTS, part] = half(ring.total(part))

        self.ring(unit, 1).start()
        ring.settle()

    def last_copy(self, unit):
        s, c = place()
        near = lax.rem(lax.div(s, 4), 2)
        ring = self.ring(unit, 1)
        sems = [s.at[unit, 2, 0] for s in (self.send, self.recv)]
        src = ring.view(1 - near, ring.here)
        return remote(src, self.last.at[unit], *sems, (s + 4 - 8 * near, c))

    def finish(self, unit):
        s, _ = place()
        near = lax.rem(lax.div(s, 4), 2)
        ring = self.ring(unit, 1)
        ring.arrive()
        ring.view(1 - near, ring.here)[...] = half(ring.total(1 - near))
        self.last_copy(unit).start()
        self.result[self.place(unit)] = ring.total(near)
        ring.settle()

    def place(self, unit):
        return pl.ds(unit * SHARE, SHARE), pl.ds(BLOCK, BLOCK)

    def out_copy(self, unit):
        cols = pl.ds(unit % 2 * BLOCK, BLOCK)
        dst = self.out[unit // 2].at[:, cols]
        return pltpu.make_async_copy(self.result.at[self.place(unit)], dst, self.out_sem.at[unit])

    def close(self, unit):
        self.last_copy(unit).wait_recv()
        if unit + SLOTS >= UNITS:
            self.last_copy(unit).wait_send()
        place = self.place(unit)
        self.result[place] = self.result[place] + full(self.last[unit])
        self.out_copy(unit).start()


class ChanSum:
    def __init__(self, part, near, far, send, recv):
        self.part, self.near, self.far, self.send, self.recv = part, near, far, send, recv
        s, c = place()
        self.high, self.core = lax.div(c, 2), lax.rem(c, 2)
        self.beside, self.across = (s, c + 1 - 2 * self.core), (s, lax.rem(c + 2, 4))

    def near_copy(self, high):
        return remote(
            self.part.at[high * 2 + 1 - self.core], self.near.at[high],
            self.send.at[high], self.recv.at[high], self.beside,
        )

    def far_copy(self):
        return remote(
            self.part.at[(1 - self.high) * 2 + self.core], self.far,
            self.send.at[2], self.recv.at[2], self.across,
        )

    def start(self):
        for high in range(2):
            self.near_copy(high).start()

    def onward(self):
        for high in range(2):
            self.near_copy(high).wait()
        other = 1 - self.high
        slot = other * 2 + self.core
        self.part[slot] = half(full(self.part[slot]) + full(self.near[other]))
        self.far_copy().start()

    def arrive(self):
        self.far_copy().wait()

    def total(self, rows):
        mine = full(self.part[self.high * 2 + self.core, rows])
        return mine + full(self.near[self.high, rows]) + full(self.far[rows])


class PairSum:
    def __init__(self, part, got, send, recv):
        self.part, self.got, self.send, self.recv = part, got, send, recv
        s, c = place()
        self.targets = (s, c + 1 - 2 * lax.rem(c, 2)), (s, lax.rem(c + 2, 4))

    def copy(self, step):
        return remote(
            self.part.at[step], self.got.at[step],
            self.send.at[step], self.recv.at[step], self.targets[step],
        )

    def start(self, values):
        self.part[0] = values
        self.copy(0).start()

    def onward(self):
        self.copy(0).wait()
        self.part[1] = half(full(self.part[0]) + full(self.got[0]))
        self.copy(1).start()

    def finish(self):
        self.copy(1).wait()
        return full(self.part[1]) + full(self.got[1])


class SeqSum:
    def __init__(self, slots, send, recv):
        self.slots, self.send, self.recv = slots, send, recv

    def copy(self, axis, step):
        mine = self.slots.at[axis, axis_place(axis)]
        return remote(
            mine, mine, self.send.at[axis, step], self.recv.at[axis, step],
            axis_peer(axis, step),
        )

    def pair_copy(self):
        s, c = place()
        near = lax.rem(lax.div(s, 4), 2)
        mine = self.slots.at[2, near]
        return remote(
            mine, mine, self.send.at[2, 1], self.recv.at[2, 1], (s + 4 - 8 * near, c)
        )

    def start(self, values):
        self.slots[0, axis_place(0)] = values
        for step in range(1, 4):
            self.copy(0, step).start()

    def take(self, axis):
        for step in range(1, 4):
            self.copy(axis, step).wait()
        return (self.slots[axis, 0] + self.slots[axis, 1]) + (
            self.slots[axis, 2] + self.slots[axis, 3]
        )

    def second(self):
        self.slots[1, axis_place(1)] = self.take(0)
        for step in range(1, 4):
            self.copy(1, step).start()

    def third(self):
        s, _ = place()
        self.slots[2, lax.rem(lax.div(s, 4), 2)] = self.take(1)
        self.pair_copy().start()

    def finish(self):
        self.pair_copy().wait()
        return self.slots[2, 0] + self.slots[2, 1]


def layer(
    x, og, f1, f2, scale, shift, gain, wg_hbm, wu_hbm, wd_hbm,
    layer_out, input_grad, one_grad, two_grad, scale_grad, shift_grad, gain_grad, down_out, gate_out, up_out,
    wg, wu, wd, cot, flipped, wm, normed, gate_pre, up_pre, hidden, gate_back, up_back,
    inv, dots, first_cols, seqmix, back_cols, first_back, src, big_two,
    sum_near, sum_far, own, mid, early_one, late_one, early_two, late_two, last,
    one_part, one_got, two_part, two_got, slots,
    w_sem, swap_send, swap_recv, gs, gr, hs, hr, grad_send, grad_recv, sum_send, sum_recv,
    dot_send, dot_recv, pair_send, pair_recv, vec_send, vec_recv, out_sem,
):
    s, c = place()
    greet()
    top, low = pl.ds(0, 256), pl.ds(256, 256)
    lows, highs = pl.ds(0, BLOCK), pl.ds(BLOCK, BLOCK)
    swap = lambda k: (swap_send.at[k], swap_recv.at[k])
    weights = [
        pltpu.make_async_copy(a, b, w_sem.at[k])
        for k, (a, b) in enumerate(((wg_hbm, wg), (wu_hbm, wu), (wd_hbm, wd)))
    ]
    for copy in weights:
        copy.start()
    src[0] = half(interleaved(dot(f1[0], x[top]), dot(f1[1], x[low])))
    greeted()
    swap_start(src.at[0], first_cols, *swap(0))
    for piece in range(PIECES):
        cot[c, pl.ds(piece * PIECE, PIECE)] = half(inside(og, piece))
    for piece in range(EARLY):
        gather_start(cot, piece, hs, hr)
    big_two[0] = spread_two(f2[...])
    big_two[1] = big_two[0].T
    swap_wait(src.at[0], first_cols, *swap(0))
    src[1] = half(dot(big_two[0], first_cols[...]))
    swap_start(src.at[1], seqmix, *swap(1))
    for piece in range(EARLY):
        gather_forward(cot, piece, hs, hr)
    swap_wait(src.at[1], seqmix, *swap(1))
    for piece in range(PIECES):
        rows = pl.ds(piece * PIECE, PIECE)
        xf = inside(x, piece)
        opening = jax.nn.sigmoid(xf * scale[...] + shift[...])
        wm[c, rows] = half(xf + opening * full(seqmix[rows]))
        gather_start(wm, piece, gs, gr)
    for piece in range(EARLY, PIECES):
        gather_start(cot, piece, hs, hr)
    for piece in range(PIECES):
        gather_forward(wm, piece, gs, gr)
    for copy in weights:
        copy.wait()

    def norm_rows(part):
        for piece in (2 * part, 2 * part + 1):
            gather_finish(wm, piece, gs, gr)

        @pl.loop(0, 4)
        def _(k):
            rows = pl.ds(pl.multiple_of(part * 256 + k * 64, 64), 64)
            blocks = [full(wm[chan, rows]) for chan in range(4)]
            squares = sum(jnp.sum(b * b, axis=1, keepdims=True) for b in blocks)
            scaled = lax.rsqrt(squares / (4 * BLOCK) + 1e-05)
            inv[rows] = jnp.broadcast_to(scaled, (64, 128))
            for chan in range(4):
                normed[chan, rows] = half(blocks[chan] * scaled * gain[chan])

    def expand(part, k):
        rows, cols = pl.ds(part * 256, 256), pl.ds(k * BLOCK, BLOCK)
        gate = up = 0.0
        for chan in range(4):
            deep = pl.ds(chan * BLOCK, BLOCK)
            gate = gate + dot(normed[chan, rows], wg[deep, cols])
            up = up + dot(normed[chan, rows], wu[deep, cols])
        gate_pre[rows, cols] = gate
        up_pre[rows, cols] = up
        hidden[rows, cols] = half(gate * jax.nn.sigmoid(gate) * up)

    norm_rows(0)
    expand(0, 0)
    expand(0, 1)
    norm_rows(1)
    expand(1, 0)
    for piece in range(EARLY, PIECES):
        gather_forward(cot, piece, hs, hr)
    for piece in range(PIECES):
        gather_finish(cot, piece, hs, hr)
    for k in range(4):
        flipped[pl.ds(k * BLOCK, BLOCK), :] = cot[k].T
    grads = Grads(
        own, mid, (early_one, late_one, early_two, late_two, last), (grad_send, grad_recv),
        gate_pre, (down_out, gate_out, up_out), out_sem,
    )
    grads.multiply(0, flipped, hidden[:, lows])
    expand(1, 1)
    grads.multiply(1, flipped, hidden[:, highs])
    for k in range(4):
        flipped[pl.ds(k * BLOCK, BLOCK), :] = normed[k].T

    for part in range(2):
        rows = pl.ds(part * 256, 256)
        products = 0.0
        for k in range(2):
            cols = pl.ds(k * BLOCK, BLOCK)
            hidden_grad = 0.0
            for chan in range(4):
                deep = pl.ds(chan * BLOCK, BLOCK)
                hidden_grad = hidden_grad + dot_rows(cot[chan, rows], wd[cols, deep])
            gate, up = gate_pre[rows, cols], up_pre[rows, cols]
            s_gate = jax.nn.sigmoid(gate)
            back = half(hidden_grad * up * s_gate * (1.0 + gate * (1.0 - s_gate)))
            gate_back[rows, cols] = back
            products = products + jnp.sum(full(back) * gate, axis=1, keepdims=True)
            back = half(hidden_grad * gate * s_gate)
            up_back[rows, cols] = back
            products = products + jnp.sum(full(back) * up, axis=1, keepdims=True)
        turned = jnp.broadcast_to(products, (256, 128)).T
        dots[c, :, rows] = turned[:8]
    dot_copies = [
        remote(dots.at[c], dots.at[c], dot_send.at[k], dot_recv.at[k], (s, lax.rem(c + k, 4)))
        for k in range(1, 4)
    ]
    for copy in dot_copies:
        copy.start()
    grads.middle(0, 0)
    grads.middle(1, 0)
    grads.multiply(2, flipped, gate_back[:, lows])
    grads.multiply(3, flipped, gate_back[:, highs])

    @pl.loop(0, 4)
    def _(chan):
        rows = pl.ds(pl.multiple_of(chan * BLOCK, BLOCK), BLOCK)
        back = dot_rows(gate_back[...], wg[rows, :]) + dot_rows(up_back[...], wu[rows, :])
        normed[chan] = half(back)

    back_sum = ChanSum(
        normed, sum_near.at[0], sum_far.at[0], sum_send.at[0], sum_recv.at[0]
    )
    back_sum.start()
    for chan in range(4):
        cols = pl.ds(chan * BLOCK, BLOCK)
        cot[chan] = half(dot(hidden[...], wd[:, cols]))
    back_sum.onward()
    out_sum = ChanSum(cot, sum_near.at[1], sum_far.at[1], sum_send.at[1], sum_recv.at[1])
    out_sum.start()
    grads.turn(0)
    grads.turn(1)
    grads.multiply(4, flipped, up_back[:, lows])
    grads.multiply(5, flipped, up_back[:, highs])
    grads.middle(2, 0)
    grads.middle(3, 0)
    for copy in dot_copies:
        copy.wait()
    row_total = (dots[0] + dots[1]) + (dots[2] + dots[3])
    up_pre[:, pl.ds(0, 128)] = jnp.broadcast_to(row_total[:1], (128, ROWS)).T

    back_sum.arrive()
    sums = [0.0, 0.0, 0.0]
    for piece in range(PIECES):
        rows = pl.ds(piece * PIECE, PIECE)
        normed_grad = back_sum.total(rows)
        scaled, total = inv[rows][:, :1], up_pre[rows, pl.ds(0, 128)][:, :1]
        mixed, xf = full(wm[c, rows]), inside(x, piece)
        mixed_grad = inside(og, piece) + scaled * gain[c] * normed_grad
        mixed_grad = mixed_grad - mixed * (scaled * scaled * total / (4 * BLOCK))
        opening = jax.nn.sigmoid(xf * scale[...] + shift[...])
        src[0, rows] = half(mixed_grad * opening)
        pre_grad = mixed_grad * full(seqmix[rows]) * opening * (1.0 - opening)
        gate_pre[rows, lows] = mixed_grad + pre_grad * scale[...]
        for k, term in enumerate((pre_grad * xf, pre_grad, normed_grad * mixed * scaled)):
            sums[k] = sums[k] + jnp.sum(term, axis=0, keepdims=True)
    swap_start(src.at[0], back_cols, *swap(2))
    out_sum.onward()
    vector_sum = SeqSum(slots, vec_send, vec_recv)
    row, _ = index_pair((8, BLOCK))
    vector_sum.start(
        jnp.where(row == 0, sums[0], jnp.where(row == 1, sums[1], jnp.where(row == 2, sums[2], 0.0)))
    )
    grads.middle(0, 1)
    grads.middle(1, 1)
    swap_wait(src.at[0], back_cols, *swap(2))
    src[1] = half(dot(big_two[1], back_cols[...]))
    swap_start(src.at[1], first_back, *swap(3))
    vector_sum.second()
    two_sum = PairSum(two_part, two_got, pair_send.at[0], pair_recv.at[0])
    two_sum.start(gather_two(dot_rows(back_cols[...], first_cols[...])))
    grads.finish(0)
    grads.finish(1)
    grads.middle(4, 0)
    grads.middle(5, 0)
    grads.turn(2)
    grads.turn(3)
    two_sum.onward()
    vector_sum.third()
    swap_wait(src.at[1], first_back, *swap(3))
    one_sum = PairSum(one_part, one_got, pair_send.at[1], pair_recv.at[1])
    blocks = [half(b) for b in deal(full(first_back[...]))]
    one_sum.start(
        jnp.concatenate(
            [half(dot_rows(blocks[0], x[top])), half(dot_rows(blocks[1], x[low]))], axis=0
        )
    )
    grads.middle(2, 1)
    grads.middle(3, 1)
    kept = deal(gate_pre[:, lows])
    for k, rows in enumerate((top, low)):
        hidden[rows, highs] = half(kept[k] + dot(f1[k].T, blocks[k]))
    outs = [
        pltpu.make_async_copy(a, b, out_sem.at[UNITS + k])
        for k, (a, b) in enumerate(
            (
                (hidden.at[:, highs], input_grad),
                (hidden.at[:, lows], layer_out),
                (up_pre.at[:, pl.ds(BLOCK, 256)], one_grad),
            )
        )
    ]
    outs[0].start()
    out_sum.arrive()
    plain_out = deal(full(wm[c]) + out_sum.total(pl.ds(0, ROWS)))
    hidden[top, lows] = half(plain_out[0])
    hidden[low, lows] = half(plain_out[1])
    outs[1].start()
    one_sum.onward()
    grads.turn(4)
    grads.turn(5)
    grads.finish(2)
    grads.finish(3)
    grads.middle(4, 1)
    grads.middle(5, 1)
    two_grad[...] = two_sum.finish()
    vector = vector_sum.finish()
    scale_grad[...], shift_grad[...], gain_grad[...] = vector[0:1], vector[1:2], vector[2:3]
    up_pre[:, pl.ds(BLOCK, 256)] = one_sum.finish()
    outs[2].start()
    for unit in range(4):
        grads.close(unit)
    grads.finish(4)
    grads.finish(5)
    grads.close(4)
    grads.close(5)
    for copy in outs:
        copy.wait()
    for unit in range(UNITS):
        grads.out_copy(unit).wait()


def hand_over(*refs):
    for src, dst in zip(refs[:OUTPUTS], refs[OUTPUTS:]):
        dst[...] = src[...]


def on_device(
    layer_in, factor_one, factor_two, gate_scale, gate_shift, norm_gain, w_gate, w_up, w_down, out_grad
):
    vmem, away = pl.BlockSpec(memory_space=pltpu.VMEM), pl.BlockSpec(memory_space=pl.ANY)
    bf, f32 = jnp.bfloat16, jnp.float32
    dma = pltpu.SemaphoreType.DMA
    square = pltpu.VMEM((ROWS, BLOCK), bf)
    whole = pltpu.VMEM((4, ROWS, BLOCK), bf)
    flipped = pltpu.VMEM((4 * BLOCK, ROWS), bf)
    wide = pltpu.VMEM((ROWS, HIDDEN), bf)
    wide_float = pltpu.VMEM((ROWS, HIDDEN), f32)
    out = jax.ShapeDtypeStruct
    outs = pl.pallas_call(
        layer,
        out_shape=(
            out((ROWS, BLOCK), bf),
            out((ROWS, BLOCK), bf),
            out((2 * 256, 256), f32),
            out((ROWS, 64), f32),
            out((1, BLOCK), f32),
            out((1, BLOCK), f32),
            out((1, BLOCK), f32),
            out((SHARE, HIDDEN), f32),
            out((SHARE, HIDDEN), f32),
            out((SHARE, HIDDEN), f32),
        ),
        in_specs=[vmem] * 7 + [away] * 3,
        out_specs=(away,) * 3 + (vmem,) * 4 + (away,) * 3,
        scratch_shapes=[
            pltpu.VMEM((4 * BLOCK, HIDDEN), bf),
            pltpu.VMEM((4 * BLOCK, HIDDEN), bf),
            pltpu.VMEM((HIDDEN, 4 * BLOCK), bf),
            whole, flipped, whole, whole,
            wide_float, wide_float, wide, wide, wide,
            pltpu.VMEM((ROWS, 128), f32),
            pltpu.VMEM((4, 8, ROWS), f32),
            square, square, square, square,
            pltpu.VMEM((2, ROWS, BLOCK), bf),
            pltpu.VMEM((2, ROWS, BLOCK), bf),
            pltpu.VMEM((2, 2, ROWS, BLOCK), bf),
            pltpu.VMEM((2, ROWS, BLOCK), bf),
            pltpu.VMEM((SLOTS, 2, 4, 4, SHARE, BLOCK), bf),
            pltpu.VMEM((SLOTS, 2, 4, SHARE, BLOCK), bf),
            pltpu.VMEM((UNITS, 2, 4, SHARE, BLOCK), bf),
            pltpu.VMEM((UNITS, 2, 2, 4, SHARE, BLOCK), bf),
            pltpu.VMEM((UNITS, 2, SHARE, BLOCK), bf),
            pltpu.VMEM((UNITS, 2, 2, SHARE, BLOCK), bf),
            pltpu.VMEM((UNITS, SHARE, BLOCK), bf),
            pltpu.VMEM((2, 2 * 256, 256), bf),
            pltpu.VMEM((2, 2 * 256, 256), bf),
            pltpu.VMEM((2, ROWS, 64), bf),
            pltpu.VMEM((2, ROWS, 64), bf),
            pltpu.VMEM((3, 4, 8, BLOCK), f32),
            dma((3,)),
            dma((4,)), dma((4,)),
            dma((3, PIECES)), dma((3, PIECES)), dma((3, PIECES)), dma((3, PIECES)),
            dma((UNITS, 3, 6)), dma((UNITS, 3, 6)),
            dma((2, 3)), dma((2, 3)),
            dma((4,)), dma((4,)),
            dma((2, 2)), dma((2, 2)),
            dma((3, 4)), dma((3, 4)),
            dma((UNITS + 3,)),
        ],
        compiler_params=pltpu.CompilerParams(
            collective_id=0, has_side_effects=True, vmem_limit_bytes=VMEM_LIMIT
        ),
        name="layer",
    )(
        layer_in, out_grad, factor_one, factor_two,
        gate_scale.reshape(1, -1), gate_shift.reshape(1, -1), norm_gain.reshape(4, 1, -1),
        w_gate, w_up, w_down,
    )
    shapes = [(ROWS, BLOCK, bf), (ROWS, BLOCK, bf), (2 * 256, 256, f32), (ROWS, 64, f32)]
    shapes = [out(s[:-1], s[-1]) for s in shapes] + [out((1, BLOCK), f32)] * 3
    shapes += [out((SHARE, HIDDEN), f32)] * 3
    results = pl.pallas_call(
        hand_over,
        out_shape=tuple(shapes),
        in_specs=[vmem] * OUTPUTS,
        out_specs=(vmem,) * OUTPUTS,
        name="hand_over",
    )(*outs)
    layer_out, input_grad, one_grad, two_grad, scale_grad, shift_grad, gain_grad, *grads = results
    return (
        layer_out,
        input_grad,
        one_grad.reshape(factor_one.shape),
        two_grad.reshape(factor_two.shape),
        scale_grad.reshape(-1),
        shift_grad.reshape(-1),
        gain_grad.reshape(-1),
        grads[1],
        grads[2],
        grads[0].T,
    )


def solution(mesh):
    return jax.shard_map(
        on_device,
        mesh=mesh,
        in_specs=(
            P("seq", "chan"),
            P("seq", None, None),
            P("seq", None, None),
            P("chan"),
            P("chan"),
            P(),
            P(None, "chan"),
            P(None, "chan"),
            P("chan", None),
            P("seq", "chan"),
        ),
        out_specs=(
            P("seq", "chan"),
            P("seq", "chan"),
            P("seq", None, None),
            P("seq", None, None),
            P("chan"),
            P("chan"),
            P("chan"),
            P("seq", "chan"),
            P("seq", "chan"),
            P("chan", "seq"),
        ),
        check_vma=False,
    )
```

```python
import jax
import jax.numpy as jnp
from jax import lax
from jax.experimental import pallas as pl
from jax.experimental.pallas import tpu as pltpu
from jax.sharding import PartitionSpec as P

MESH = pl.DeviceIdType.MESH
PARTS = 32
SLAB = 16
ROWS = 512
PIECES = 4
PIECE = ROWS // PIECES
BLOCK = 512
HIDDEN = 1024
UNITS = 10
SLOTS = 4
SHARE = 64
EARLY = 2
SOON = 2
OUTPUTS = 10
VMEM_LIMIT = 67000000


def interleaved(low, high):
    rows, width = low.shape
    pair = [part.reshape(rows // 8, 8, width) for part in (low, high)]
    return jnp.stack(pair, axis=1).reshape(2 * rows, width)


def inside(ref, piece):
    return interleaved(
        *[full(ref[pl.ds(k * 256 + piece * PIECE // 2, PIECE // 2)]) for k in range(2)]
    )


def deal(whole):
    parts = whole.reshape(PARTS, 2, 8, whole.shape[1])
    return [parts[:, k].reshape(ROWS // 2, whole.shape[1]) for k in range(2)]


def dot(a, b):
    return jnp.dot(a, b, preferred_element_type=jnp.float32)


def dot_rows(a, b):
    return lax.dot_general(a, b, (((1,), (1,)), ((), ())), preferred_element_type=jnp.float32)


def half(values):
    return values.astype(jnp.bfloat16)


def full(values):
    return values.astype(jnp.float32)


def place():
    return lax.axis_index("seq"), lax.axis_index("chan")


def greet():
    s, c = place()
    barrier = pltpu.get_barrier_semaphore()

    def greet_seq(step, carry):
        target = (lax.rem(s + step, PARTS), c)
        pl.semaphore_signal(barrier, inc=1, device_id=target, device_id_type=MESH)
        return carry

    lax.fori_loop(1, PARTS, greet_seq, 0)
    for step in range(1, 4):
        target = (s, lax.rem(c + step, 4))
        pl.semaphore_signal(barrier, inc=1, device_id=target, device_id_type=MESH)


def greeted():
    pl.semaphore_wait(pltpu.get_barrier_semaphore(), PARTS - 1 + 3)


def slab(index):
    return pl.ds(pl.multiple_of(index * SLAB, SLAB), SLAB)


def swap_start(src, dst, send, recv):
    s, c = place()

    def one(step, carry):
        target = lax.rem(s + step, PARTS)
        pltpu.make_async_remote_copy(
            src_ref=src.at[slab(target)],
            dst_ref=dst.at[slab(s)],
            send_sem=send,
            recv_sem=recv,
            device_id=(target, c),
            device_id_type=MESH,
        ).start()
        return carry

    lax.fori_loop(1, PARTS, one, 0)
    dst[slab(s), :] = src[slab(s), :]


def swap_wait(src, dst, send, recv):
    s, c = place()
    most = pl.ds(0, ROWS - SLAB)
    pltpu.make_async_remote_copy(
        src_ref=src.at[most],
        dst_ref=dst.at[most],
        send_sem=send,
        recv_sem=recv,
        device_id=(lax.rem(s + 1, PARTS), c),
        device_id_type=MESH,
    ).wait()


def chan_copy(buf, owner, piece, lane, send, recv, target):
    part = buf.at[owner, pl.ds(piece * PIECE, PIECE)]
    return pltpu.make_async_remote_copy(
        src_ref=part,
        dst_ref=part,
        send_sem=send.at[lane, piece],
        recv_sem=recv.at[lane, piece],
        device_id=target,
        device_id_type=MESH,
    )


def gather_copy(buf, piece, lane, send, recv):
    s, c = place()
    across, beside = lax.rem(c + 2, 4), c + 1 - 2 * lax.rem(c, 2)
    owner = across if lane == 2 else c
    target = across if lane == 0 else beside
    return chan_copy(buf, owner, piece, lane, send, recv, (s, target))


def gather_start(buf, piece, send, recv):
    gather_copy(buf, piece, 0, send, recv).start()
    gather_copy(buf, piece, 1, send, recv).start()


def gather_forward(buf, piece, send, recv):
    gather_copy(buf, piece, 0, send, recv).wait_recv()
    gather_copy(buf, piece, 2, send, recv).start()


def gather_finish(buf, piece, send, recv):
    gather_copy(buf, piece, 1, send, recv).wait()
    gather_copy(buf, piece, 2, send, recv).wait()
    gather_copy(buf, piece, 0, send, recv).wait_send()


def bits(mask):
    return half(mask.astype(jnp.float32))


def index_pair(shape):
    return lax.broadcasted_iota(jnp.int32, shape, 0), lax.broadcasted_iota(jnp.int32, shape, 1)


def same_place():
    row, col = index_pair((ROWS, ROWS))
    return jnp.bitwise_and(row, 7) == jnp.bitwise_and(col, 7)


def reorder(transposed):
    row, col = index_pair((ROWS, ROWS))
    if transposed:
        row, col = col, row
    return bits(col == jnp.bitwise_and(row, 7) * 64 + lax.shift_right_logical(row, 3))


def widen():
    row, col = index_pair((64, ROWS))
    return bits(row == lax.shift_right_logical(col, 3))


def spread_two(f2):
    wide = half(dot(f2.reshape(ROWS, 64), widen()))
    return half(jnp.where(same_place(), dot(reorder(False), wide), 0.0))


def gather_two(product):
    tall = half(dot_rows(half(jnp.where(same_place(), product, 0.0)), widen()))
    return half(dot(reorder(True), tall))


def remote(src, dst, send, recv, target):
    return pltpu.make_async_remote_copy(
        src_ref=src, dst_ref=dst, send_sem=send, recv_sem=recv,
        device_id=target, device_id_type=MESH,
    )


def axis_place(axis):
    s, _ = place()
    return lax.rem(s, 4) if axis == 0 else lax.div(s, 8)


def axis_peer(axis, step):
    s, c = place()
    here = axis_place(axis)
    there = lax.rem(here + step, 4)
    return s + (there - here) * (1 if axis == 0 else 8), c


class Ring:
    def __init__(self, view, early, late, send, recv, axis):
        self.view, self.early, self.late = view, early, late
        self.send, self.recv = send, recv
        self.here = axis_place(axis)
        self.ahead, self.behind = axis_peer(axis, 1), axis_peer(axis, 3)

    def copy(self, index):
        after, across, before = [lax.rem(self.here + k, 4) for k in (1, 2, 3)]
        src, dst, target = (
            lambda: (self.view(0, across), self.early.at[0], self.ahead),
            lambda: (self.view(1, across), self.early.at[1], self.behind),
            lambda: (self.view(1, after), self.late.at[0, 1], self.ahead),
            lambda: (self.view(0, before), self.late.at[1, 0], self.behind),
            lambda: (self.view(0, after), self.late.at[0, 0], self.ahead),
            lambda: (self.view(1, before), self.late.at[1, 1], self.behind),
        )[index]()
        return remote(src, dst, self.send.at[index], self.recv.at[index], target)

    def start(self):
        for index in range(4):
            self.copy(index).start()

    def middle(self):
        after, before = lax.rem(self.here + 1, 4), lax.rem(self.here + 3, 4)
        for way, owner in ((0, after), (1, before)):
            self.copy(way).wait_recv()
            mine = self.view(way, owner)
            mine[...] = half(full(mine[...]) + full(self.early[way]))
            self.copy(4 + way).start()

    def arrive(self):
        for index in range(2, 6):
            self.copy(index).wait_recv()

    def total(self, part):
        return full(self.view(part, self.here)[...]) + (
            full(self.late[0, part]) + full(self.late[1, part])
        )

    def settle(self):
        for index in range(6):
            self.copy(index).wait_send()


class Grads:
    def __init__(self, own, families, got, sems, result, out, out_sem):
        self.own, self.families, self.got = own, families, got
        self.send, self.recv = sems
        self.result, self.out, self.out_sem = result, out, out_sem
        s, c = place()
        self.near = lax.rem(lax.div(s, 4), 2)
        self.partner = (s + 4 - 8 * self.near, c)

    def where(self, unit):
        if unit in (6, 7):
            return 2, unit - 6
        return (0, unit) if unit < 2 else (1, unit - 2 if unit < 6 else unit - 4)

    def ring(self, unit, stage):
        family, k = self.where(unit)
        early_one, late_one, early_two, late_two, mid = self.families[family][:5]
        sems = [s.at[unit, stage] for s in (self.send, self.recv)]
        first, own = unit % 2, self.own
        if stage == 1:
            view = lambda part, owner: mid.at[k, part, owner]
            return Ring(view, early_two.at[k], late_two.at[k], *sems, 1 - first)
        cols = pl.ds(k % 2 * 256, 256)
        if family == 0:
            view = lambda part, owner: own.at[2 + unit, part, owner]
        elif family == 1:
            view = lambda part, owner: own.at[1 + k // 4 * 2, part, owner, :, :, cols]
        elif first == 0:
            view = lambda part, owner: own.at[0, self.near, :, owner, pl.ds(part * 32, 32), cols]
        else:
            view = lambda part, owner: own.at[0, self.near, owner, :, pl.ds(part * 32, 32), cols]
        return Ring(view, early_one.at[k], late_one.at[k], *sems, first)

    def multiply(self, slot, left, right, mode):
        own = self.own
        for z in range(4):
            tile = half(dot(left[pl.ds(z * 512, 512), :], right).reshape(2, 4, SHARE, BLOCK))
            if mode == 0:
                own[slot, :, :, z] = tile
            elif mode == 1:
                own[slot, :, z] = tile
            else:
                own[slot, :, :, z, :, pl.ds(0, 256)] = tile[..., :256]
                own[slot, :, z, :, :, pl.ds(256, 256)] = tile[..., 256:]

    def start(self, unit):
        self.ring(unit, 0).start()

    def middle(self, unit, stage):
        self.ring(unit, stage).middle()

    def meet_copy(self):
        src = self.own.at[0, 1 - self.near]
        return remote(src, self.got, self.send.at[6, 2, 0], self.recv.at[6, 2, 0], self.partner)

    def meet(self):
        self.meet_copy().wait()

        @pl.loop(0, 4)
        def _(z):
            mine = self.own.at[0, self.near, z]
            mine[...] = half(full(mine[...]) + full(self.got[z]))

        self.start(6)
        self.start(7)

    def turn(self, unit):
        family, k = self.where(unit)
        mid = self.families[family][4]
        ring = self.ring(unit, 0)
        ring.arrive()

        @pl.loop(0, 2)
        def _(part):
            mid[k, part] = half(ring.total(part))

        self.ring(unit, 1).start()
        ring.settle()

    def last_copy(self, unit):
        family, k = self.where(unit)
        ring = self.ring(unit, 1)
        sems = [s.at[unit, 2, 0] for s in (self.send, self.recv)]
        src = ring.view(1 - self.near, ring.here)
        return remote(src, self.families[family][5].at[k], *sems, self.partner)

    def finish(self, unit):
        ring = self.ring(unit, 1)
        ring.arrive()
        if unit not in (6, 7):
            ring.view(1 - self.near, ring.here)[...] = half(ring.total(1 - self.near))
            self.last_copy(unit).start()
            self.result[self.place(unit)] = ring.total(self.near)
        else:
            rows, cols = self.place(unit)
            for part in range(2):
                self.result[pl.ds(rows.start + part * 32, 32), cols] = ring.total(part)
            self.out_copy(unit).start()
        ring.settle()

    def close(self, unit):
        family, k = self.where(unit)
        self.last_copy(unit).wait()
        place = self.place(unit)
        self.result[place] = self.result[place] + full(self.families[family][5][k])
        self.out_copy(unit).start()

    def place(self, unit):
        family, k = self.where(unit)
        if family == 0:
            return pl.ds(unit * SHARE, SHARE), pl.ds(BLOCK, BLOCK)
        block = 5 if family == 2 else 2 + k // 2
        return pl.ds(block * SHARE, SHARE), pl.ds(BLOCK + k % 2 * 256, 256)

    def out_copy(self, unit):
        family, k = self.where(unit)
        if family == 0:
            dst = self.out[1].at[:, pl.ds(k * BLOCK, BLOCK)]
        else:
            which, base = (0, 0) if family == 2 else ((2, 0), (0, BLOCK), (2, BLOCK))[k // 2]
            dst = self.out[which].at[:, pl.ds(base + k % 2 * 256, 256)]
        return pltpu.make_async_copy(self.result.at[self.place(unit)], dst, self.out_sem.at[unit])


class ChanSum:
    def __init__(self, part, near, far, send, recv):
        self.part, self.near, self.far, self.send, self.recv = part, near, far, send, recv
        s, c = place()
        self.high, self.core = lax.div(c, 2), lax.rem(c, 2)
        self.beside, self.across = (s, c + 1 - 2 * self.core), (s, lax.rem(c + 2, 4))

    def near_copy(self, high):
        return remote(
            self.part.at[high * 2 + 1 - self.core], self.near.at[high],
            self.send.at[high], self.recv.at[high], self.beside,
        )

    def far_copy(self):
        return remote(
            self.part.at[(1 - self.high) * 2 + self.core], self.far,
            self.send.at[2], self.recv.at[2], self.across,
        )

    def start(self):
        for high in range(2):
            self.near_copy(high).start()

    def onward(self):
        for high in range(2):
            self.near_copy(high).wait()
        other = 1 - self.high
        slot = other * 2 + self.core
        self.part[slot] = half(full(self.part[slot]) + full(self.near[other]))
        self.far_copy().start()

    def arrive(self):
        self.far_copy().wait()

    def total(self, rows):
        mine = full(self.part[self.high * 2 + self.core, rows])
        return mine + full(self.near[self.high, rows]) + full(self.far[rows])


class PairSum:
    def __init__(self, part, got, send, recv):
        self.part, self.got, self.send, self.recv = part, got, send, recv
        s, c = place()
        self.targets = (s, c + 1 - 2 * lax.rem(c, 2)), (s, lax.rem(c + 2, 4))

    def copy(self, step):
        return remote(
            self.part.at[step], self.got.at[step],
            self.send.at[step], self.recv.at[step], self.targets[step],
        )

    def start(self, values):
        self.part[0] = values
        self.copy(0).start()

    def onward(self):
        self.copy(0).wait()
        self.part[1] = half(full(self.part[0]) + full(self.got[0]))
        self.copy(1).start()

    def finish(self):
        self.copy(1).wait()
        return full(self.part[1]) + full(self.got[1])


class SeqSum:
    def __init__(self, slots, send, recv):
        self.slots, self.send, self.recv = slots, send, recv

    def copy(self, axis, step):
        mine = self.slots.at[axis, axis_place(axis)]
        return remote(
            mine, mine, self.send.at[axis, step], self.recv.at[axis, step],
            axis_peer(axis, step),
        )

    def pair_copy(self):
        s, c = place()
        near = lax.rem(lax.div(s, 4), 2)
        mine = self.slots.at[2, near]
        return remote(
            mine, mine, self.send.at[2, 1], self.recv.at[2, 1], (s + 4 - 8 * near, c)
        )

    def start(self, values):
        self.slots[0, axis_place(0)] = values
        for step in range(1, 4):
            self.copy(0, step).start()

    def take(self, axis):
        for step in range(1, 4):
            self.copy(axis, step).wait()
        return (self.slots[axis, 0] + self.slots[axis, 1]) + (
            self.slots[axis, 2] + self.slots[axis, 3]
        )

    def second(self):
        self.slots[1, axis_place(1)] = self.take(0)
        for step in range(1, 4):
            self.copy(1, step).start()

    def third(self):
        s, _ = place()
        self.slots[2, lax.rem(lax.div(s, 4), 2)] = self.take(1)
        self.pair_copy().start()

    def finish(self):
        self.pair_copy().wait()
        return self.slots[2, 0] + self.slots[2, 1]


def layer(
    x, og, f1, f2, scale, shift, gain, wg_hbm, wu_hbm, wd_hbm,
    layer_out, input_grad, one_grad, two_grad, scale_grad, shift_grad, gain_grad, down_out, gate_out, up_out,
    wg, wu, wd, cot, flipped, wm, normed, gate_pre, up_pre, hidden, gate_back, up_back,
    inv, dots, first_cols, seqmix, back_cols, first_back, src, big_two,
    sum_near, sum_far, own, got,
    early_one, late_one, early_two, late_two, mid, last,
    early_one5, late_one5, early_two5, late_two5, mid5, last5,
    early_one4, late_one4, early_two4, late_two4, mid4,
    one_part, one_got, two_part, two_got, slots,
    w_sem, swap_send, swap_recv, gs, gr, hs, hr, grad_send, grad_recv, sum_send, sum_recv,
    dot_send, dot_recv, pair_send, pair_recv, vec_send, vec_recv, out_sem,
):
    s, c = place()
    greet()
    top, low = pl.ds(0, 256), pl.ds(256, 256)
    lows, highs = pl.ds(0, BLOCK), pl.ds(BLOCK, BLOCK)
    swap = lambda k: (swap_send.at[k], swap_recv.at[k])
    weights = [
        pltpu.make_async_copy(a, b, w_sem.at[k])
        for k, (a, b) in enumerate(((wg_hbm, wg), (wu_hbm, wu), (wd_hbm, wd)))
    ]
    for copy in weights:
        copy.start()
    src[0] = half(interleaved(dot(f1[0], x[top]), dot(f1[1], x[low])))
    greeted()
    swap_start(src.at[0], first_cols, *swap(0))
    for piece in range(PIECES):
        cot[c, pl.ds(piece * PIECE, PIECE)] = half(inside(og, piece))
    for piece in range(EARLY):
        gather_start(cot, piece, hs, hr)
    big_two[0] = spread_two(f2[...])
    big_two[1] = big_two[0].T
    swap_wait(src.at[0], first_cols, *swap(0))
    src[1] = half(dot(big_two[0], first_cols[...]))
    swap_start(src.at[1], seqmix, *swap(1))
    for piece in range(EARLY, SOON):
        gather_start(cot, piece, hs, hr)
    for piece in range(EARLY):
        gather_forward(cot, piece, hs, hr)
    swap_wait(src.at[1], seqmix, *swap(1))
    for piece in range(PIECES):
        rows = pl.ds(piece * PIECE, PIECE)
        xf = inside(x, piece)
        opening = jax.nn.sigmoid(xf * scale[...] + shift[...])
        wm[c, rows] = half(xf + opening * full(seqmix[rows]))
        gather_start(wm, piece, gs, gr)
    for piece in range(SOON, PIECES):
        gather_start(cot, piece, hs, hr)
    for piece in range(EARLY, SOON):
        gather_forward(cot, piece, hs, hr)
    for piece in range(PIECES):
        gather_forward(wm, piece, gs, gr)
    for copy in weights:
        copy.wait()

    def norm_rows(part):
        for piece in (2 * part, 2 * part + 1):
            gather_finish(wm, piece, gs, gr)

        @pl.loop(0, 4)
        def _(k):
            rows = pl.ds(pl.multiple_of(part * 256 + k * 64, 64), 64)
            blocks = [full(wm[chan, rows]) for chan in range(4)]
            squares = sum(jnp.sum(b * b, axis=1, keepdims=True) for b in blocks)
            scaled = lax.rsqrt(squares / (4 * BLOCK) + 1e-05)
            inv[rows] = jnp.broadcast_to(scaled, (64, 128))
            for chan in range(4):
                normed[chan, rows] = half(blocks[chan] * scaled * gain[chan])

    def expand(part, k):
        rows, cols = pl.ds(part * 256, 256), pl.ds(k * BLOCK, BLOCK)
        gate = up = 0.0
        for chan in range(4):
            deep = pl.ds(chan * BLOCK, BLOCK)
            gate = gate + dot(normed[chan, rows], wg[deep, cols])
            up = up + dot(normed[chan, rows], wu[deep, cols])
        gate_pre[rows, cols] = gate
        up_pre[rows, cols] = up
        hidden[rows, cols] = half(gate * jax.nn.sigmoid(gate) * up)

    norm_rows(0)
    expand(0, 0)
    expand(0, 1)
    norm_rows(1)
    expand(1, 0)
    for piece in range(SOON, PIECES):
        gather_forward(cot, piece, hs, hr)
    for piece in range(PIECES):
        gather_finish(cot, piece, hs, hr)
    for k in range(4):
        flipped[pl.ds(k * BLOCK, BLOCK), :] = cot[k].T
    grads = Grads(
        own,
        (
            (early_one, late_one, early_two, late_two, mid, last),
            (early_one5, late_one5, early_two5, late_two5, mid5, last5),
            (early_one4, late_one4, early_two4, late_two4, mid4),
        ),
        got,
        (grad_send, grad_recv),
        gate_pre, (down_out, gate_out, up_out), out_sem,
    )
    grads.multiply(0, flipped, hidden[:, lows], 1)
    grads.meet_copy().start()
    expand(1, 1)
    grads.multiply(1, flipped, hidden[:, highs], 2)
    grads.start(4)
    grads.start(5)
    for k in range(4):
        flipped[pl.ds(k * BLOCK, BLOCK), :] = normed[k].T

    for part in range(2):
        rows = pl.ds(part * 256, 256)
        products = 0.0
        for k in range(2):
            cols = pl.ds(k * BLOCK, BLOCK)
            hidden_grad = 0.0
            for chan in range(4):
                deep = pl.ds(chan * BLOCK, BLOCK)
                hidden_grad = hidden_grad + dot_rows(cot[chan, rows], wd[cols, deep])
            gate, up = gate_pre[rows, cols], up_pre[rows, cols]
            s_gate = jax.nn.sigmoid(gate)
            back = half(hidden_grad * up * s_gate * (1.0 + gate * (1.0 - s_gate)))
            gate_back[rows, cols] = back
            products = products + jnp.sum(full(back) * gate, axis=1, keepdims=True)
            back = half(hidden_grad * gate * s_gate)
            up_back[rows, cols] = back
            products = products + jnp.sum(full(back) * up, axis=1, keepdims=True)
        turned = jnp.broadcast_to(products, (256, 128)).T
        dots[c, :, rows] = turned[:8]
    dot_copies = [
        remote(dots.at[c], dots.at[c], dot_send.at[k], dot_recv.at[k], (s, lax.rem(c + k, 4)))
        for k in range(1, 4)
    ]
    for copy in dot_copies:
        copy.start()
    grads.middle(4, 0)
    grads.middle(5, 0)
    grads.multiply(2, flipped, gate_back[:, lows], 0)
    grads.start(0)
    grads.multiply(3, flipped, gate_back[:, highs], 1)
    grads.start(1)

    @pl.loop(0, 4)
    def _(chan):
        rows = pl.ds(pl.multiple_of(chan * BLOCK, BLOCK), BLOCK)
        back = dot_rows(gate_back[...], wg[rows, :]) + dot_rows(up_back[...], wu[rows, :])
        normed[chan] = half(back)

    back_sum = ChanSum(
        normed, sum_near.at[0], sum_far.at[0], sum_send.at[0], sum_recv.at[0]
    )
    back_sum.start()
    grads.turn(4)
    grads.turn(5)
    grads.multiply(1, flipped, up_back[:, lows], 2)
    grads.start(2)
    grads.start(3)
    back_sum.onward()
    grads.middle(0, 0)
    grads.middle(1, 0)
    for chan in range(4):
        cols = pl.ds(chan * BLOCK, BLOCK)
        cot[chan] = half(dot(hidden[...], wd[:, cols]))
    out_sum = ChanSum(cot, sum_near.at[1], sum_far.at[1], sum_send.at[1], sum_recv.at[1])
    out_sum.start()
    for copy in dot_copies:
        copy.wait()
    row_total = (dots[0] + dots[1]) + (dots[2] + dots[3])
    up_pre[:, pl.ds(0, 128)] = jnp.broadcast_to(row_total[:1], (128, ROWS)).T
    grads.meet()
    grads.middle(4, 1)
    grads.middle(5, 1)
    grads.turn(1)
    grads.multiply(3, flipped, up_back[:, highs], 2)
    grads.start(8)
    grads.start(9)
    grads.middle(2, 0)
    grads.middle(3, 0)

    back_sum.arrive()
    sums = [0.0, 0.0, 0.0]
    for piece in range(PIECES):
        rows = pl.ds(piece * PIECE, PIECE)
        normed_grad = back_sum.total(rows)
        scaled, total = inv[rows][:, :1], up_pre[rows, pl.ds(0, 128)][:, :1]
        mixed, xf = full(wm[c, rows]), inside(x, piece)
        mixed_grad = inside(og, piece) + scaled * gain[c] * normed_grad
        mixed_grad = mixed_grad - mixed * (scaled * scaled * total / (4 * BLOCK))
        opening = jax.nn.sigmoid(xf * scale[...] + shift[...])
        src[0, rows] = half(mixed_grad * opening)
        pre_grad = mixed_grad * full(seqmix[rows]) * opening * (1.0 - opening)
        gate_pre[rows, lows] = mixed_grad + pre_grad * scale[...]
        for k, term in enumerate((pre_grad * xf, pre_grad, normed_grad * mixed * scaled)):
            sums[k] = sums[k] + jnp.sum(term, axis=0, keepdims=True)
    swap_start(src.at[0], back_cols, *swap(2))
    out_sum.onward()
    vector_sum = SeqSum(slots, vec_send, vec_recv)
    row, _ = index_pair((8, BLOCK))
    vector_sum.start(
        jnp.where(row == 0, sums[0], jnp.where(row == 1, sums[1], jnp.where(row == 2, sums[2], 0.0)))
    )
    grads.middle(6, 0)
    grads.middle(7, 0)
    grads.finish(4)
    grads.finish(5)
    grads.turn(0)
    grads.middle(8, 0)
    grads.middle(9, 0)
    swap_wait(src.at[0], back_cols, *swap(2))
    src[1] = half(dot(big_two[1], back_cols[...]))
    swap_start(src.at[1], first_back, *swap(3))
    vector_sum.second()
    two_sum = PairSum(two_part, two_got, pair_send.at[0], pair_recv.at[0])
    two_sum.start(gather_two(dot_rows(back_cols[...], first_cols[...])))
    grads.middle(1, 1)
    grads.turn(6)
    grads.turn(7)
    grads.middle(0, 1)
    grads.turn(2)
    grads.turn(3)
    grads.close(4)
    grads.close(5)
    out_sum.arrive()
    plain_out = deal(full(wm[c]) + out_sum.total(pl.ds(0, ROWS)))
    hidden[top, lows] = half(plain_out[0])
    hidden[low, lows] = half(plain_out[1])
    outs = [
        pltpu.make_async_copy(a, b, out_sem.at[UNITS + k])
        for k, (a, b) in enumerate(
            (
                (hidden.at[:, highs], input_grad),
                (hidden.at[:, lows], layer_out),
                (up_pre.at[:, pl.ds(BLOCK, 256)], one_grad),
            )
        )
    ]
    outs[1].start()
    two_sum.onward()
    vector_sum.third()
    grads.turn(8)
    grads.turn(9)
    swap_wait(src.at[1], first_back, *swap(3))
    one_sum = PairSum(one_part, one_got, pair_send.at[1], pair_recv.at[1])
    blocks = [half(b) for b in deal(full(first_back[...]))]
    one_sum.start(
        jnp.concatenate(
            [half(dot_rows(blocks[0], x[top])), half(dot_rows(blocks[1], x[low]))], axis=0
        )
    )
    grads.middle(2, 1)
    grads.middle(3, 1)
    grads.middle(8, 1)
    grads.middle(9, 1)
    kept = deal(gate_pre[:, lows])
    for k, rows in enumerate((top, low)):
        hidden[rows, highs] = half(kept[k] + dot(f1[k].T, blocks[k]))
    outs[0].start()
    one_sum.onward()
    grads.middle(6, 1)
    grads.middle(7, 1)
    grads.finish(0)
    grads.finish(1)
    two_grad[...] = two_sum.finish()
    vector = vector_sum.finish()
    scale_grad[...], shift_grad[...], gain_grad[...] = vector[0:1], vector[1:2], vector[2:3]
    grads.finish(2)
    grads.finish(3)
    grads.finish(8)
    grads.finish(9)
    grads.finish(6)
    grads.finish(7)
    up_pre[:, pl.ds(BLOCK, 256)] = one_sum.finish()
    outs[2].start()
    for unit in (0, 1, 2, 3, 8, 9):
        grads.close(unit)
    for copy in outs:
        copy.wait()
    for unit in range(UNITS):
        grads.out_copy(unit).wait()


def hand_over(*refs):
    for src, dst in zip(refs[:OUTPUTS], refs[OUTPUTS:]):
        dst[...] = src[...]


def on_device(
    layer_in, factor_one, factor_two, gate_scale, gate_shift, norm_gain, w_gate, w_up, w_down, out_grad
):
    vmem, away = pl.BlockSpec(memory_space=pltpu.VMEM), pl.BlockSpec(memory_space=pl.ANY)
    bf, f32 = jnp.bfloat16, jnp.float32
    dma = pltpu.SemaphoreType.DMA
    square = pltpu.VMEM((ROWS, BLOCK), bf)
    whole = pltpu.VMEM((4, ROWS, BLOCK), bf)
    flipped = pltpu.VMEM((4 * BLOCK, ROWS), bf)
    wide = pltpu.VMEM((ROWS, HIDDEN), bf)
    wide_float = pltpu.VMEM((ROWS, HIDDEN), f32)
    out = jax.ShapeDtypeStruct
    outs = pl.pallas_call(
        layer,
        out_shape=(
            out((ROWS, BLOCK), bf),
            out((ROWS, BLOCK), bf),
            out((2 * 256, 256), f32),
            out((ROWS, 64), f32),
            out((1, BLOCK), f32),
            out((1, BLOCK), f32),
            out((1, BLOCK), f32),
            out((SHARE, HIDDEN), f32),
            out((SHARE, HIDDEN), f32),
            out((SHARE, HIDDEN), f32),
        ),
        in_specs=[vmem] * 7 + [away] * 3,
        out_specs=(away,) * 3 + (vmem,) * 4 + (away,) * 3,
        scratch_shapes=[
            pltpu.VMEM((4 * BLOCK, HIDDEN), bf),
            pltpu.VMEM((4 * BLOCK, HIDDEN), bf),
            pltpu.VMEM((HIDDEN, 4 * BLOCK), bf),
            whole, flipped, whole, whole,
            wide_float, wide_float, wide, wide, wide,
            pltpu.VMEM((ROWS, 128), f32),
            pltpu.VMEM((4, 8, ROWS), f32),
            square, square, square, square,
            pltpu.VMEM((2, ROWS, BLOCK), bf),
            pltpu.VMEM((2, ROWS, BLOCK), bf),
            pltpu.VMEM((2, 2, ROWS, BLOCK), bf),
            pltpu.VMEM((2, ROWS, BLOCK), bf),
            pltpu.VMEM((SLOTS, 2, 4, 4, SHARE, BLOCK), bf),
            pltpu.VMEM((4, 4, SHARE, BLOCK), bf),
            pltpu.VMEM((2, 2, 4, SHARE, BLOCK), bf),
            pltpu.VMEM((2, 2, 2, 4, SHARE, BLOCK), bf),
            pltpu.VMEM((2, 2, SHARE, BLOCK), bf),
            pltpu.VMEM((2, 2, 2, SHARE, BLOCK), bf),
            pltpu.VMEM((2, 2, 4, SHARE, BLOCK), bf),
            pltpu.VMEM((2, SHARE, BLOCK), bf),
            pltpu.VMEM((6, 2, 4, SHARE, 256), bf),
            pltpu.VMEM((6, 2, 2, 4, SHARE, 256), bf),
            pltpu.VMEM((6, 2, SHARE, 256), bf),
            pltpu.VMEM((6, 2, 2, SHARE, 256), bf),
            pltpu.VMEM((6, 2, 4, SHARE, 256), bf),
            pltpu.VMEM((6, SHARE, 256), bf),
            pltpu.VMEM((2, 2, 4, SHARE // 2, 256), bf),
            pltpu.VMEM((2, 2, 2, 4, SHARE // 2, 256), bf),
            pltpu.VMEM((2, 2, SHARE // 2, 256), bf),
            pltpu.VMEM((2, 2, 2, SHARE // 2, 256), bf),
            pltpu.VMEM((2, 2, 4, SHARE // 2, 256), bf),
            pltpu.VMEM((2, 2 * 256, 256), bf),
            pltpu.VMEM((2, 2 * 256, 256), bf),
            pltpu.VMEM((2, ROWS, 64), bf),
            pltpu.VMEM((2, ROWS, 64), bf),
            pltpu.VMEM((3, 4, 8, BLOCK), f32),
            dma((3,)),
            dma((4,)), dma((4,)),
            dma((3, PIECES)), dma((3, PIECES)), dma((3, PIECES)), dma((3, PIECES)),
            dma((UNITS, 3, 6)), dma((UNITS, 3, 6)),
            dma((2, 3)), dma((2, 3)),
            dma((4,)), dma((4,)),
            dma((2, 2)), dma((2, 2)),
            dma((3, 4)), dma((3, 4)),
            dma((UNITS + 3,)),
        ],
        compiler_params=pltpu.CompilerParams(
            collective_id=0, has_side_effects=True, vmem_limit_bytes=VMEM_LIMIT
        ),
        name="layer",
    )(
        layer_in, out_grad, factor_one, factor_two,
        gate_scale.reshape(1, -1), gate_shift.reshape(1, -1), norm_gain.reshape(4, 1, -1),
        w_gate, w_up, w_down,
    )
    shapes = [(ROWS, BLOCK, bf), (ROWS, BLOCK, bf), (2 * 256, 256, f32), (ROWS, 64, f32)]
    shapes = [out(s[:-1], s[-1]) for s in shapes] + [out((1, BLOCK), f32)] * 3
    shapes += [out((SHARE, HIDDEN), f32)] * 3
    results = pl.pallas_call(
        hand_over,
        out_shape=tuple(shapes),
        in_specs=[vmem] * OUTPUTS,
        out_specs=(vmem,) * OUTPUTS,
        name="hand_over",
    )(*outs)
    layer_out, input_grad, one_grad, two_grad, scale_grad, shift_grad, gain_grad, *grads = results
    return (
        layer_out,
        input_grad,
        one_grad.reshape(factor_one.shape),
        two_grad.reshape(factor_two.shape),
        scale_grad.reshape(-1),
        shift_grad.reshape(-1),
        gain_grad.reshape(-1),
        grads[1],
        grads[2],
        grads[0].T,
    )


def solution(mesh):
    return jax.shard_map(
        on_device,
        mesh=mesh,
        in_specs=(
            P("seq", "chan"),
            P("seq", None, None),
            P("seq", None, None),
            P("chan"),
            P("chan"),
            P(),
            P(None, "chan"),
            P(None, "chan"),
            P("chan", None),
            P("seq", "chan"),
        ),
        out_specs=(
            P("seq", "chan"),
            P("seq", "chan"),
            P("seq", None, None),
            P("seq", None, None),
            P("chan"),
            P("chan"),
            P("chan"),
            P("seq", "chan"),
            P("seq", "chan"),
            P("chan", "seq"),
        ),
        check_vma=False,
    )
```

```python
import jax
import jax.numpy as jnp
from jax import lax
from jax.experimental import pallas as pl
from jax.experimental.pallas import tpu as pltpu
from jax.sharding import PartitionSpec as P

MESH = pl.DeviceIdType.MESH
PARTS = 32
SLAB = 16
ROWS = 512
PIECES = 4
PIECE = ROWS // PIECES
BLOCK = 512
HIDDEN = 1024
UNITS = 10
SLOTS = 4
SHARE = 64
EARLY = 2
SOON = 2
OUTPUTS = 10
VMEM_LIMIT = 67000000


def interleaved(low, high):
    rows, width = low.shape
    pair = [part.reshape(rows // 8, 8, width) for part in (low, high)]
    return jnp.stack(pair, axis=1).reshape(2 * rows, width)


def inside(ref, piece):
    return interleaved(
        *[full(ref[pl.ds(k * 256 + piece * PIECE // 2, PIECE // 2)]) for k in range(2)]
    )


def deal(whole):
    parts = whole.reshape(PARTS, 2, 8, whole.shape[1])
    return [parts[:, k].reshape(ROWS // 2, whole.shape[1]) for k in range(2)]


def dot(a, b):
    return jnp.dot(a, b, preferred_element_type=jnp.float32)


def dot_rows(a, b):
    return lax.dot_general(a, b, (((1,), (1,)), ((), ())), preferred_element_type=jnp.float32)


def half(values):
    return values.astype(jnp.bfloat16)


def full(values):
    return values.astype(jnp.float32)


def place():
    return lax.axis_index("seq"), lax.axis_index("chan")


def greet():
    s, c = place()
    barrier = pltpu.get_barrier_semaphore()

    def greet_seq(step, carry):
        target = (lax.rem(s + step, PARTS), c)
        pl.semaphore_signal(barrier, inc=1, device_id=target, device_id_type=MESH)
        return carry

    lax.fori_loop(1, PARTS, greet_seq, 0)
    for step in range(1, 4):
        target = (s, lax.rem(c + step, 4))
        pl.semaphore_signal(barrier, inc=1, device_id=target, device_id_type=MESH)


def greeted():
    pl.semaphore_wait(pltpu.get_barrier_semaphore(), PARTS - 1 + 3)


def slab(index):
    return pl.ds(pl.multiple_of(index * SLAB, SLAB), SLAB)


def swap_start(src, dst, send, recv):
    s, c = place()

    def one(step, carry):
        target = lax.rem(s + step, PARTS)
        pltpu.make_async_remote_copy(
            src_ref=src.at[slab(target)],
            dst_ref=dst.at[slab(s)],
            send_sem=send,
            recv_sem=recv,
            device_id=(target, c),
            device_id_type=MESH,
        ).start()
        return carry

    lax.fori_loop(1, PARTS, one, 0)
    dst[slab(s), :] = src[slab(s), :]


def swap_wait(src, dst, send, recv):
    s, c = place()
    most = pl.ds(0, ROWS - SLAB)
    pltpu.make_async_remote_copy(
        src_ref=src.at[most],
        dst_ref=dst.at[most],
        send_sem=send,
        recv_sem=recv,
        device_id=(lax.rem(s + 1, PARTS), c),
        device_id_type=MESH,
    ).wait()


def chan_copy(buf, owner, piece, lane, send, recv, target):
    part = buf.at[owner, pl.ds(piece * PIECE, PIECE)]
    return pltpu.make_async_remote_copy(
        src_ref=part,
        dst_ref=part,
        send_sem=send.at[lane, piece],
        recv_sem=recv.at[lane, piece],
        device_id=target,
        device_id_type=MESH,
    )


def gather_copy(buf, piece, lane, send, recv):
    s, c = place()
    across, beside = lax.rem(c + 2, 4), c + 1 - 2 * lax.rem(c, 2)
    owner = across if lane == 2 else c
    target = across if lane == 0 else beside
    return chan_copy(buf, owner, piece, lane, send, recv, (s, target))


def gather_start(buf, piece, send, recv):
    gather_copy(buf, piece, 0, send, recv).start()
    gather_copy(buf, piece, 1, send, recv).start()


def gather_forward(buf, piece, send, recv):
    gather_copy(buf, piece, 0, send, recv).wait_recv()
    gather_copy(buf, piece, 2, send, recv).start()


def gather_finish(buf, piece, send, recv):
    gather_copy(buf, piece, 1, send, recv).wait()
    gather_copy(buf, piece, 2, send, recv).wait()
    gather_copy(buf, piece, 0, send, recv).wait_send()


def bits(mask):
    return half(mask.astype(jnp.float32))


def index_pair(shape):
    return lax.broadcasted_iota(jnp.int32, shape, 0), lax.broadcasted_iota(jnp.int32, shape, 1)


def same_place():
    row, col = index_pair((ROWS, ROWS))
    return jnp.bitwise_and(row, 7) == jnp.bitwise_and(col, 7)


def reorder(transposed):
    row, col = index_pair((ROWS, ROWS))
    if transposed:
        row, col = col, row
    return bits(col == jnp.bitwise_and(row, 7) * 64 + lax.shift_right_logical(row, 3))


def widen():
    row, col = index_pair((64, ROWS))
    return bits(row == lax.shift_right_logical(col, 3))


def spread_two(f2):
    wide = half(dot(f2.reshape(ROWS, 64), widen()))
    return half(jnp.where(same_place(), dot(reorder(False), wide), 0.0))


def gather_two(product):
    tall = half(dot_rows(half(jnp.where(same_place(), product, 0.0)), widen()))
    return half(dot(reorder(True), tall))


def remote(src, dst, send, recv, target):
    return pltpu.make_async_remote_copy(
        src_ref=src, dst_ref=dst, send_sem=send, recv_sem=recv,
        device_id=target, device_id_type=MESH,
    )


def axis_place(axis):
    s, _ = place()
    return lax.rem(s, 4) if axis == 0 else lax.div(s, 8)


def axis_peer(axis, step):
    s, c = place()
    here = axis_place(axis)
    there = lax.rem(here + step, 4)
    return s + (there - here) * (1 if axis == 0 else 8), c


class Ring:
    def __init__(self, view, early, late, send, recv, axis):
        self.view, self.early, self.late = view, early, late
        self.send, self.recv = send, recv
        self.here = axis_place(axis)
        self.ahead, self.behind = axis_peer(axis, 1), axis_peer(axis, 3)

    def copy(self, index):
        after, across, before = [lax.rem(self.here + k, 4) for k in (1, 2, 3)]
        src, dst, target = (
            lambda: (self.view(0, across), self.early.at[0], self.ahead),
            lambda: (self.view(1, across), self.early.at[1], self.behind),
            lambda: (self.view(1, after), self.late.at[0, 1], self.ahead),
            lambda: (self.view(0, before), self.late.at[1, 0], self.behind),
            lambda: (self.view(0, after), self.late.at[0, 0], self.ahead),
            lambda: (self.view(1, before), self.late.at[1, 1], self.behind),
        )[index]()
        return remote(src, dst, self.send.at[index], self.recv.at[index], target)

    def start(self):
        for index in range(4):
            self.copy(index).start()

    def middle(self):
        after, before = lax.rem(self.here + 1, 4), lax.rem(self.here + 3, 4)
        for way, owner in ((0, after), (1, before)):
            self.copy(way).wait_recv()
            mine = self.view(way, owner)
            mine[...] = half(full(mine[...]) + full(self.early[way]))
            self.copy(4 + way).start()

    def arrive(self):
        for index in range(2, 6):
            self.copy(index).wait_recv()

    def total(self, part):
        return full(self.view(part, self.here)[...]) + (
            full(self.late[0, part]) + full(self.late[1, part])
        )

    def settle(self):
        for index in range(6):
            self.copy(index).wait_send()


class Grads:
    def __init__(self, own, families, got, sems, result, out, out_sem):
        self.own, self.families, self.got = own, families, got
        self.send, self.recv = sems
        self.result, self.out, self.out_sem = result, out, out_sem
        s, c = place()
        self.near = lax.rem(lax.div(s, 4), 2)
        self.partner = (s + 4 - 8 * self.near, c)

    def where(self, unit):
        if unit in (6, 7):
            return 2, unit - 6
        return (0, unit) if unit < 2 else (1, unit - 2 if unit < 6 else unit - 4)

    def ring(self, unit, stage):
        family, k = self.where(unit)
        early_one, late_one, early_two, late_two, mid = self.families[family][:5]
        sems = [s.at[unit, stage] for s in (self.send, self.recv)]
        first, own = unit % 2, self.own
        if stage == 1:
            view = lambda part, owner: mid.at[k, part, owner]
            return Ring(view, early_two.at[k], late_two.at[k], *sems, 1 - first)
        cols = pl.ds(k % 2 * 256, 256)
        if family == 0:
            view = lambda part, owner: own.at[2 + unit, part, owner]
        elif family == 1:
            view = lambda part, owner: own.at[1 + k // 4 * 2, part, owner, :, :, cols]
        elif first == 0:
            view = lambda part, owner: own.at[0, self.near, :, owner, pl.ds(part * 32, 32), cols]
        else:
            view = lambda part, owner: own.at[0, self.near, owner, :, pl.ds(part * 32, 32), cols]
        return Ring(view, early_one.at[k], late_one.at[k], *sems, first)

    def multiply(self, slot, left, right, mode):
        own = self.own
        for z in range(4):
            tile = half(dot(left[pl.ds(z * 512, 512), :], right).reshape(2, 4, SHARE, BLOCK))
            if mode == 0:
                own[slot, :, :, z] = tile
            elif mode == 1:
                own[slot, :, z] = tile
            else:
                own[slot, :, :, z, :, pl.ds(0, 256)] = tile[..., :256]
                own[slot, :, z, :, :, pl.ds(256, 256)] = tile[..., 256:]

    def start(self, unit):
        self.ring(unit, 0).start()

    def middle(self, unit, stage):
        self.ring(unit, stage).middle()

    def meet_copy(self):
        src = self.own.at[0, 1 - self.near]
        return remote(src, self.got, self.send.at[6, 2, 0], self.recv.at[6, 2, 0], self.partner)

    def meet(self):
        self.meet_copy().wait()

        @pl.loop(0, 4)
        def _(z):
            mine = self.own.at[0, self.near, z]
            mine[...] = half(full(mine[...]) + full(self.got[z]))

        self.start(6)
        self.start(7)

    def turn(self, unit):
        family, k = self.where(unit)
        mid = self.families[family][4]
        ring = self.ring(unit, 0)
        ring.arrive()

        @pl.loop(0, 2)
        def _(part):
            mid[k, part] = half(ring.total(part))

        self.ring(unit, 1).start()
        ring.settle()

    def last_copy(self, unit):
        family, k = self.where(unit)
        ring = self.ring(unit, 1)
        sems = [s.at[unit, 2, 0] for s in (self.send, self.recv)]
        src = ring.view(1 - self.near, ring.here)
        return remote(src, self.families[family][5].at[k], *sems, self.partner)

    def finish(self, unit):
        ring = self.ring(unit, 1)
        ring.arrive()
        if unit not in (6, 7):
            ring.view(1 - self.near, ring.here)[...] = half(ring.total(1 - self.near))
            self.last_copy(unit).start()
            self.result[self.place(unit)] = ring.total(self.near)
        else:
            rows, cols = self.place(unit)
            for part in range(2):
                self.result[pl.ds(rows.start + part * 32, 32), cols] = ring.total(part)
            self.out_copy(unit).start()
        ring.settle()

    def close(self, unit):
        family, k = self.where(unit)
        self.last_copy(unit).wait()
        place = self.place(unit)
        self.result[place] = self.result[place] + full(self.families[family][5][k])
        self.out_copy(unit).start()

    def place(self, unit):
        family, k = self.where(unit)
        if family == 0:
            return pl.ds(unit * SHARE, SHARE), pl.ds(BLOCK, BLOCK)
        block = 5 if family == 2 else 2 + k // 2
        return pl.ds(block * SHARE, SHARE), pl.ds(BLOCK + k % 2 * 256, 256)

    def out_copy(self, unit):
        family, k = self.where(unit)
        if family == 0:
            dst = self.out[1].at[:, pl.ds(k * BLOCK, BLOCK)]
        else:
            which, base = (0, 0) if family == 2 else ((2, 0), (0, BLOCK), (2, BLOCK))[k // 2]
            dst = self.out[which].at[:, pl.ds(base + k % 2 * 256, 256)]
        return pltpu.make_async_copy(self.result.at[self.place(unit)], dst, self.out_sem.at[unit])


class ChanSum:
    def __init__(self, part, near, far, send, recv):
        self.part, self.near, self.far, self.send, self.recv = part, near, far, send, recv
        s, c = place()
        self.high, self.core = lax.div(c, 2), lax.rem(c, 2)
        self.beside, self.across = (s, c + 1 - 2 * self.core), (s, lax.rem(c + 2, 4))

    def near_copy(self, high):
        return remote(
            self.part.at[high * 2 + 1 - self.core], self.near.at[high],
            self.send.at[high], self.recv.at[high], self.beside,
        )

    def far_copy(self):
        return remote(
            self.part.at[(1 - self.high) * 2 + self.core], self.far,
            self.send.at[2], self.recv.at[2], self.across,
        )

    def start(self):
        for high in range(2):
            self.near_copy(high).start()

    def onward(self):
        for high in range(2):
            self.near_copy(high).wait()
        other = 1 - self.high
        slot = other * 2 + self.core
        self.part[slot] = half(full(self.part[slot]) + full(self.near[other]))
        self.far_copy().start()

    def arrive(self):
        self.far_copy().wait()

    def total(self, rows):
        mine = full(self.part[self.high * 2 + self.core, rows])
        return mine + full(self.near[self.high, rows]) + full(self.far[rows])


class PairSum:
    def __init__(self, part, got, send, recv):
        self.part, self.got, self.send, self.recv = part, got, send, recv
        s, c = place()
        self.targets = (s, c + 1 - 2 * lax.rem(c, 2)), (s, lax.rem(c + 2, 4))

    def copy(self, step):
        return remote(
            self.part.at[step], self.got.at[step],
            self.send.at[step], self.recv.at[step], self.targets[step],
        )

    def start(self, values):
        self.part[0] = values
        self.copy(0).start()

    def onward(self):
        self.copy(0).wait()
        self.part[1] = half(full(self.part[0]) + full(self.got[0]))
        self.copy(1).start()

    def finish(self):
        self.copy(1).wait()
        return full(self.part[1]) + full(self.got[1])


class SeqSum:
    def __init__(self, slots, send, recv):
        self.slots, self.send, self.recv = slots, send, recv

    def copy(self, axis, step):
        mine = self.slots.at[axis, axis_place(axis)]
        return remote(
            mine, mine, self.send.at[axis, step], self.recv.at[axis, step],
            axis_peer(axis, step),
        )

    def pair_copy(self):
        s, c = place()
        near = lax.rem(lax.div(s, 4), 2)
        mine = self.slots.at[2, near]
        return remote(
            mine, mine, self.send.at[2, 1], self.recv.at[2, 1], (s + 4 - 8 * near, c)
        )

    def start(self, values):
        self.slots[0, axis_place(0)] = values
        for step in range(1, 4):
            self.copy(0, step).start()

    def take(self, axis):
        for step in range(1, 4):
            self.copy(axis, step).wait()
        return (self.slots[axis, 0] + self.slots[axis, 1]) + (
            self.slots[axis, 2] + self.slots[axis, 3]
        )

    def second(self):
        self.slots[1, axis_place(1)] = self.take(0)
        for step in range(1, 4):
            self.copy(1, step).start()

    def third(self):
        s, _ = place()
        self.slots[2, lax.rem(lax.div(s, 4), 2)] = self.take(1)
        self.pair_copy().start()

    def finish(self):
        self.pair_copy().wait()
        return self.slots[2, 0] + self.slots[2, 1]


def layer(
    x, og, f1, f2, scale, shift, gain, wg_hbm, wu_hbm, wd_hbm,
    layer_out, input_grad, one_grad, two_grad, scale_grad, shift_grad, gain_grad, down_out, gate_out, up_out,
    wg, wu, wd, cot, flipped, wm, normed, gate_pre, up_pre, hidden, gate_back, up_back,
    inv, dots, first_cols, seqmix, back_cols, first_back, src, big_two,
    sum_near, sum_far, own, got,
    early_one, late_one, early_two, late_two, mid, last,
    early_one5, late_one5, early_two5, late_two5, mid5, last5,
    early_one4, late_one4, early_two4, late_two4, mid4,
    one_part, one_got, two_part, two_got, slots,
    w_sem, swap_send, swap_recv, gs, gr, hs, hr, grad_send, grad_recv, sum_send, sum_recv,
    dot_send, dot_recv, pair_send, pair_recv, vec_send, vec_recv, out_sem,
):
    s, c = place()
    greet()
    top, low = pl.ds(0, 256), pl.ds(256, 256)
    lows, highs = pl.ds(0, BLOCK), pl.ds(BLOCK, BLOCK)
    swap = lambda k: (swap_send.at[k], swap_recv.at[k])
    weights = [
        pltpu.make_async_copy(a, b, w_sem.at[k])
        for k, (a, b) in enumerate(((wg_hbm, wg), (wu_hbm, wu), (wd_hbm, wd)))
    ]
    for copy in weights:
        copy.start()
    src[0] = half(interleaved(dot(f1[0], x[top]), dot(f1[1], x[low])))
    greeted()
    swap_start(src.at[0], first_cols, *swap(0))
    for piece in range(PIECES):
        cot[c, pl.ds(piece * PIECE, PIECE)] = half(inside(og, piece))
    for piece in range(EARLY):
        gather_start(cot, piece, hs, hr)
    big_two[0] = spread_two(f2[...])
    big_two[1] = big_two[0].T
    swap_wait(src.at[0], first_cols, *swap(0))
    src[1] = half(dot(big_two[0], first_cols[...]))
    swap_start(src.at[1], seqmix, *swap(1))
    for piece in range(EARLY, SOON):
        gather_start(cot, piece, hs, hr)
    for piece in range(EARLY):
        gather_forward(cot, piece, hs, hr)
    swap_wait(src.at[1], seqmix, *swap(1))
    for piece in range(PIECES):
        rows = pl.ds(piece * PIECE, PIECE)
        xf = inside(x, piece)
        opening = jax.nn.sigmoid(xf * scale[...] + shift[...])
        wm[c, rows] = half(xf + opening * full(seqmix[rows]))
        gather_start(wm, piece, gs, gr)
    for piece in range(SOON, PIECES):
        gather_start(cot, piece, hs, hr)
    for piece in range(EARLY, SOON):
        gather_forward(cot, piece, hs, hr)
    for piece in range(PIECES):
        gather_forward(wm, piece, gs, gr)
    for copy in weights:
        copy.wait()

    def norm_rows(part):
        for piece in (2 * part, 2 * part + 1):
            gather_finish(wm, piece, gs, gr)

        @pl.loop(0, 4)
        def _(k):
            rows = pl.ds(pl.multiple_of(part * 256 + k * 64, 64), 64)
            blocks = [full(wm[chan, rows]) for chan in range(4)]
            squares = sum(jnp.sum(b * b, axis=1, keepdims=True) for b in blocks)
            scaled = lax.rsqrt(squares / (4 * BLOCK) + 1e-05)
            inv[rows] = jnp.broadcast_to(scaled, (64, 128))
            for chan in range(4):
                normed[chan, rows] = half(blocks[chan] * scaled * gain[chan])

    def expand(part, k):
        rows, cols = pl.ds(part * 256, 256), pl.ds(k * BLOCK, BLOCK)
        gate = up = 0.0
        for chan in range(4):
            deep = pl.ds(chan * BLOCK, BLOCK)
            gate = gate + dot(normed[chan, rows], wg[deep, cols])
            up = up + dot(normed[chan, rows], wu[deep, cols])
        gate_pre[rows, cols] = gate
        up_pre[rows, cols] = up
        hidden[rows, cols] = half(gate * jax.nn.sigmoid(gate) * up)

    norm_rows(0)
    expand(0, 0)
    expand(0, 1)
    norm_rows(1)
    expand(1, 0)
    for piece in range(SOON, PIECES):
        gather_forward(cot, piece, hs, hr)
    for piece in range(PIECES):
        gather_finish(cot, piece, hs, hr)
    for k in range(4):
        flipped[pl.ds(k * BLOCK, BLOCK), :] = cot[k].T
    grads = Grads(
        own,
        (
            (early_one, late_one, early_two, late_two, mid, last),
            (early_one5, late_one5, early_two5, late_two5, mid5, last5),
            (early_one4, late_one4, early_two4, late_two4, mid4),
        ),
        got,
        (grad_send, grad_recv),
        gate_pre, (down_out, gate_out, up_out), out_sem,
    )
    grads.multiply(0, flipped, hidden[:, lows], 1)
    grads.meet_copy().start()
    expand(1, 1)
    grads.multiply(1, flipped, hidden[:, highs], 2)
    grads.start(4)
    grads.start(5)
    for k in range(4):
        flipped[pl.ds(k * BLOCK, BLOCK), :] = normed[k].T

    for part in range(2):
        rows = pl.ds(part * 256, 256)
        products = 0.0
        for k in range(2):
            cols = pl.ds(k * BLOCK, BLOCK)
            hidden_grad = 0.0
            for chan in range(4):
                deep = pl.ds(chan * BLOCK, BLOCK)
                hidden_grad = hidden_grad + dot_rows(cot[chan, rows], wd[cols, deep])
            gate, up = gate_pre[rows, cols], up_pre[rows, cols]
            s_gate = jax.nn.sigmoid(gate)
            back = half(hidden_grad * up * s_gate * (1.0 + gate * (1.0 - s_gate)))
            gate_back[rows, cols] = back
            products = products + jnp.sum(full(back) * gate, axis=1, keepdims=True)
            back = half(hidden_grad * gate * s_gate)
            up_back[rows, cols] = back
            products = products + jnp.sum(full(back) * up, axis=1, keepdims=True)
        turned = jnp.broadcast_to(products, (256, 128)).T
        dots[c, :, rows] = turned[:8]
    dot_copies = [
        remote(dots.at[c], dots.at[c], dot_send.at[k], dot_recv.at[k], (s, lax.rem(c + k, 4)))
        for k in range(1, 4)
    ]
    for copy in dot_copies:
        copy.start()
    grads.middle(4, 0)
    grads.middle(5, 0)
    grads.multiply(2, flipped, gate_back[:, lows], 0)
    grads.start(0)
    grads.multiply(3, flipped, gate_back[:, highs], 1)
    grads.start(1)

    @pl.loop(0, 4)
    def _(chan):
        rows = pl.ds(pl.multiple_of(chan * BLOCK, BLOCK), BLOCK)
        back = dot_rows(gate_back[...], wg[rows, :]) + dot_rows(up_back[...], wu[rows, :])
        normed[chan] = half(back)

    back_sum = ChanSum(
        normed, sum_near.at[0], sum_far.at[0], sum_send.at[0], sum_recv.at[0]
    )
    back_sum.start()
    grads.turn(4)
    grads.turn(5)
    grads.multiply(1, flipped, up_back[:, lows], 2)
    grads.start(2)
    grads.start(3)
    back_sum.onward()
    grads.middle(0, 0)
    grads.middle(1, 0)
    for chan in range(4):
        cols = pl.ds(chan * BLOCK, BLOCK)
        cot[chan] = half(dot(hidden[...], wd[:, cols]))
    out_sum = ChanSum(cot, sum_near.at[1], sum_far.at[1], sum_send.at[1], sum_recv.at[1])
    out_sum.start()
    for copy in dot_copies:
        copy.wait()
    row_total = (dots[0] + dots[1]) + (dots[2] + dots[3])
    up_pre[:, pl.ds(0, 128)] = jnp.broadcast_to(row_total[:1], (128, ROWS)).T
    grads.meet()
    grads.middle(4, 1)
    grads.middle(5, 1)
    grads.turn(1)
    grads.multiply(3, flipped, up_back[:, highs], 2)
    grads.start(8)
    grads.start(9)
    grads.middle(2, 0)
    grads.middle(3, 0)

    back_sum.arrive()
    sums = [0.0, 0.0, 0.0]
    for piece in range(PIECES):
        rows = pl.ds(piece * PIECE, PIECE)
        normed_grad = back_sum.total(rows)
        scaled, total = inv[rows][:, :1], up_pre[rows, pl.ds(0, 128)][:, :1]
        mixed, xf = full(wm[c, rows]), inside(x, piece)
        mixed_grad = inside(og, piece) + scaled * gain[c] * normed_grad
        mixed_grad = mixed_grad - mixed * (scaled * scaled * total / (4 * BLOCK))
        opening = jax.nn.sigmoid(xf * scale[...] + shift[...])
        src[0, rows] = half(mixed_grad * opening)
        pre_grad = mixed_grad * full(seqmix[rows]) * opening * (1.0 - opening)
        gate_pre[rows, lows] = mixed_grad + pre_grad * scale[...]
        for k, term in enumerate((pre_grad * xf, pre_grad, normed_grad * mixed * scaled)):
            sums[k] = sums[k] + jnp.sum(term, axis=0, keepdims=True)
    swap_start(src.at[0], back_cols, *swap(2))
    out_sum.onward()
    vector_sum = SeqSum(slots, vec_send, vec_recv)
    row, _ = index_pair((8, BLOCK))
    vector_sum.start(
        jnp.where(row == 0, sums[0], jnp.where(row == 1, sums[1], jnp.where(row == 2, sums[2], 0.0)))
    )
    grads.middle(6, 0)
    grads.middle(7, 0)
    grads.finish(4)
    grads.finish(5)
    grads.turn(0)
    grads.middle(8, 0)
    grads.middle(9, 0)
    swap_wait(src.at[0], back_cols, *swap(2))
    src[1] = half(dot(big_two[1], back_cols[...]))
    swap_start(src.at[1], first_back, *swap(3))
    vector_sum.second()
    two_sum = PairSum(two_part, two_got, pair_send.at[0], pair_recv.at[0])
    two_sum.start(gather_two(dot_rows(back_cols[...], first_cols[...])))
    grads.middle(1, 1)
    grads.turn(6)
    grads.turn(7)
    grads.middle(0, 1)
    grads.turn(2)
    grads.turn(3)
    grads.close(4)
    grads.close(5)
    out_sum.arrive()
    plain_out = deal(full(wm[c]) + out_sum.total(pl.ds(0, ROWS)))
    hidden[top, lows] = half(plain_out[0])
    hidden[low, lows] = half(plain_out[1])
    outs = [
        pltpu.make_async_copy(a, b, out_sem.at[UNITS + k])
        for k, (a, b) in enumerate(
            (
                (hidden.at[:, highs], input_grad),
                (hidden.at[:, lows], layer_out),
                (up_pre.at[:, pl.ds(BLOCK, 256)], one_grad),
            )
        )
    ]
    outs[1].start()
    two_sum.onward()
    vector_sum.third()
    grads.turn(8)
    grads.turn(9)
    swap_wait(src.at[1], first_back, *swap(3))
    one_sum = PairSum(one_part, one_got, pair_send.at[1], pair_recv.at[1])
    blocks = [half(b) for b in deal(full(first_back[...]))]
    one_sum.start(
        jnp.concatenate(
            [half(dot_rows(blocks[0], x[top])), half(dot_rows(blocks[1], x[low]))], axis=0
        )
    )
    grads.middle(2, 1)
    grads.middle(3, 1)
    grads.middle(8, 1)
    grads.middle(9, 1)
    kept = deal(gate_pre[:, lows])
    for k, rows in enumerate((top, low)):
        hidden[rows, highs] = half(kept[k] + dot(f1[k].T, blocks[k]))
    outs[0].start()
    one_sum.onward()
    grads.middle(6, 1)
    grads.middle(7, 1)
    grads.finish(0)
    grads.finish(1)
    two_grad[...] = two_sum.finish()
    vector = vector_sum.finish()
    scale_grad[...], shift_grad[...], gain_grad[...] = vector[0:1], vector[1:2], vector[2:3]
    grads.finish(2)
    grads.finish(3)
    grads.finish(8)
    grads.finish(9)
    grads.finish(6)
    grads.finish(7)
    up_pre[:, pl.ds(BLOCK, 256)] = one_sum.finish()
    outs[2].start()
    for unit in (0, 1, 2, 3, 8, 9):
        grads.close(unit)
    for copy in outs:
        copy.wait()
    for unit in range(UNITS):
        grads.out_copy(unit).wait()


def hand_over(*refs):
    ins, outs = refs[:OUTPUTS], refs[OUTPUTS : 2 * OUTPUTS]
    held, sems = refs[2 * OUTPUTS : -1], refs[-1]
    taken = [
        pltpu.make_async_copy(a, b, sems.at[0, k]) for k, (a, b) in enumerate(zip(ins, held))
    ]
    given = [
        pltpu.make_async_copy(a, b, sems.at[1, k]) for k, (a, b) in enumerate(zip(held, outs))
    ]
    for copy in taken:
        copy.start()
    for first, second in zip(taken, given):
        first.wait()
        second.start()
    for copy in given:
        copy.wait()


def on_device(
    layer_in, factor_one, factor_two, gate_scale, gate_shift, norm_gain, w_gate, w_up, w_down, out_grad
):
    vmem, away = pl.BlockSpec(memory_space=pltpu.VMEM), pl.BlockSpec(memory_space=pl.ANY)
    bf, f32 = jnp.bfloat16, jnp.float32
    dma = pltpu.SemaphoreType.DMA
    square = pltpu.VMEM((ROWS, BLOCK), bf)
    whole = pltpu.VMEM((4, ROWS, BLOCK), bf)
    flipped = pltpu.VMEM((4 * BLOCK, ROWS), bf)
    wide = pltpu.VMEM((ROWS, HIDDEN), bf)
    wide_float = pltpu.VMEM((ROWS, HIDDEN), f32)
    out = jax.ShapeDtypeStruct
    outs = pl.pallas_call(
        layer,
        out_shape=(
            out((ROWS, BLOCK), bf),
            out((ROWS, BLOCK), bf),
            out((2 * 256, 256), f32),
            out((ROWS, 64), f32),
            out((1, BLOCK), f32),
            out((1, BLOCK), f32),
            out((1, BLOCK), f32),
            out((SHARE, HIDDEN), f32),
            out((SHARE, HIDDEN), f32),
            out((SHARE, HIDDEN), f32),
        ),
        in_specs=[vmem] * 7 + [away] * 3,
        out_specs=(away,) * 3 + (vmem,) * 4 + (away,) * 3,
        scratch_shapes=[
            pltpu.VMEM((4 * BLOCK, HIDDEN), bf),
            pltpu.VMEM((4 * BLOCK, HIDDEN), bf),
            pltpu.VMEM((HIDDEN, 4 * BLOCK), bf),
            whole, flipped, whole, whole,
            wide_float, wide_float, wide, wide, wide,
            pltpu.VMEM((ROWS, 128), f32),
            pltpu.VMEM((4, 8, ROWS), f32),
            square, square, square, square,
            pltpu.VMEM((2, ROWS, BLOCK), bf),
            pltpu.VMEM((2, ROWS, BLOCK), bf),
            pltpu.VMEM((2, 2, ROWS, BLOCK), bf),
            pltpu.VMEM((2, ROWS, BLOCK), bf),
            pltpu.VMEM((SLOTS, 2, 4, 4, SHARE, BLOCK), bf),
            pltpu.VMEM((4, 4, SHARE, BLOCK), bf),
            pltpu.VMEM((2, 2, 4, SHARE, BLOCK), bf),
            pltpu.VMEM((2, 2, 2, 4, SHARE, BLOCK), bf),
            pltpu.VMEM((2, 2, SHARE, BLOCK), bf),
            pltpu.VMEM((2, 2, 2, SHARE, BLOCK), bf),
            pltpu.VMEM((2, 2, 4, SHARE, BLOCK), bf),
            pltpu.VMEM((2, SHARE, BLOCK), bf),
            pltpu.VMEM((6, 2, 4, SHARE, 256), bf),
            pltpu.VMEM((6, 2, 2, 4, SHARE, 256), bf),
            pltpu.VMEM((6, 2, SHARE, 256), bf),
            pltpu.VMEM((6, 2, 2, SHARE, 256), bf),
            pltpu.VMEM((6, 2, 4, SHARE, 256), bf),
            pltpu.VMEM((6, SHARE, 256), bf),
            pltpu.VMEM((2, 2, 4, SHARE // 2, 256), bf),
            pltpu.VMEM((2, 2, 2, 4, SHARE // 2, 256), bf),
            pltpu.VMEM((2, 2, SHARE // 2, 256), bf),
            pltpu.VMEM((2, 2, 2, SHARE // 2, 256), bf),
            pltpu.VMEM((2, 2, 4, SHARE // 2, 256), bf),
            pltpu.VMEM((2, 2 * 256, 256), bf),
            pltpu.VMEM((2, 2 * 256, 256), bf),
            pltpu.VMEM((2, ROWS, 64), bf),
            pltpu.VMEM((2, ROWS, 64), bf),
            pltpu.VMEM((3, 4, 8, BLOCK), f32),
            dma((3,)),
            dma((4,)), dma((4,)),
            dma((3, PIECES)), dma((3, PIECES)), dma((3, PIECES)), dma((3, PIECES)),
            dma((UNITS, 3, 6)), dma((UNITS, 3, 6)),
            dma((2, 3)), dma((2, 3)),
            dma((4,)), dma((4,)),
            dma((2, 2)), dma((2, 2)),
            dma((3, 4)), dma((3, 4)),
            dma((UNITS + 3,)),
        ],
        compiler_params=pltpu.CompilerParams(
            collective_id=0, has_side_effects=True, vmem_limit_bytes=VMEM_LIMIT
        ),
        name="layer",
    )(
        layer_in, out_grad, factor_one, factor_two,
        gate_scale.reshape(1, -1), gate_shift.reshape(1, -1), norm_gain.reshape(4, 1, -1),
        w_gate, w_up, w_down,
    )
    shapes = [(ROWS, BLOCK, bf), (ROWS, BLOCK, bf), (2 * 256, 256, f32), (ROWS, 64, f32)]
    shapes = [out(s[:-1], s[-1]) for s in shapes] + [out((1, BLOCK), f32)] * 3
    shapes += [out((SHARE, HIDDEN), f32)] * 3
    results = pl.pallas_call(
        hand_over,
        out_shape=tuple(shapes),
        in_specs=[away] * OUTPUTS,
        out_specs=(away,) * OUTPUTS,
        scratch_shapes=[pltpu.VMEM(s.shape, s.dtype) for s in shapes] + [dma((2, OUTPUTS))],
        name="hand_over",
    )(*outs)
    layer_out, input_grad, one_grad, two_grad, scale_grad, shift_grad, gain_grad, *grads = results
    return (
        layer_out,
        input_grad,
        one_grad.reshape(factor_one.shape),
        two_grad.reshape(factor_two.shape),
        scale_grad.reshape(-1),
        shift_grad.reshape(-1),
        gain_grad.reshape(-1),
        grads[1],
        grads[2],
        grads[0].T,
    )


def solution(mesh):
    return jax.shard_map(
        on_device,
        mesh=mesh,
        in_specs=(
            P("seq", "chan"),
            P("seq", None, None),
            P("seq", None, None),
            P("chan"),
            P("chan"),
            P(),
            P(None, "chan"),
            P(None, "chan"),
            P("chan", None),
            P("seq", "chan"),
        ),
        out_specs=(
            P("seq", "chan"),
            P("seq", "chan"),
            P("seq", None, None),
            P("seq", None, None),
            P("chan"),
            P("chan"),
            P("chan"),
            P("seq", "chan"),
            P("seq", "chan"),
            P("chan", "seq"),
        ),
        check_vma=False,
    )
```
